256 devices in a mesh: frame: 8 (over z_hi, y), height: 4 (over z_lo), width: 8 (over x, core).
Axes of the slice: x: 4, y: 4, z: 8 (z_hi: 2, z_lo: 4; z = z_hi * 4 + z_lo), core: 2. Of those that a mesh axis runs over, the one named last changes fastest.
Arguments:
- queries: bfloat16 [32, 24, 48, 1536], P('frame', 'height', 'width'), may hold values from -6 to 6
- keys: bfloat16 [32, 24, 48, 1536], P('frame', 'height', 'width'), may hold values from -6 to 6
- values: bfloat16 [32, 24, 48, 1536], P('frame', 'height', 'width'), may hold values from -6 to 6
- out_grad: bfloat16 [32, 24, 48, 1536], P('frame', 'height', 'width'), may hold values from -6 to 6
- extents: int32 [12, 3], replicated, may hold values from 1 to 2, as said below
Outputs:
- attended: bfloat16 [32, 24, 48, 1536], P('frame', 'height', 'width')
- query_grad: bfloat16 [32, 24, 48, 1536], P('frame', 'height', 'width')
- key_grad: bfloat16 [32, 24, 48, 1536], P('frame', 'height', 'width')
- value_grad: bfloat16 [32, 24, 48, 1536], P('frame', 'height', 'width')
The draws below stay inside these ranges and needn't reach their ends.
Inputs may be any that keep to these rules, and one draw needn't show every extreme that they name: `extents`: some head has 2 on all three axes.
All inputs are finite; a program needn't handle non-finite values.
Results may differ from the reference program's by a relative error of at most 0.0062.
Values may be sent and summed in bfloat16 or wider, within the bound.
A program may use at most 128 MiB of HBM per device.

```python
import jax
import jax.numpy as jnp
from jax import lax

HEADS = 12
HD = 128
EXT = 2
FT = 4
HT = 6
WT = 6
NF = 32
NH = 24
NW = 48
N_FRAME = 8
N_HEIGHT = 4
N_WIDTH = 8


def draw_queries(key, part):
    own_key = jax.random.fold_in(key, 21)
    grid_shape = (NF, NH, NW, HEADS * HD)
    drawn = jax.random.truncated_normal(own_key, -6.0, 6.0, grid_shape, jnp.float32)
    return drawn.astype(jnp.bfloat16)


def draw_keys(key, part):
    own_key = jax.random.fold_in(key, 22)
    grid_shape = (NF, NH, NW, HEADS * HD)
    drawn = jax.random.truncated_normal(own_key, -6.0, 6.0, grid_shape, jnp.float32)
    return drawn.astype(jnp.bfloat16)


def draw_extents(key, part):
    key = jax.random.fold_in(key, 5)
    reaches = jax.random.randint(key, (HEADS, 3), 1, EXT + 1, dtype=jnp.int32)
    chosen = jax.random.randint(jax.random.fold_in(key, 1), (), 0, HEADS, dtype=jnp.int32)
    rows = jnp.arange(HEADS, dtype=jnp.int32)[:, None]
    return jnp.where(rows == chosen, jnp.int32(EXT), reaches).astype(jnp.int32)


def level_of(key, shape, shards, least, top_value):
    gain, own = 1.0, jax.random.fold_in(key, 6)
    for dim, blocks in shards:
        draws = jnp.exp(jax.random.uniform(jax.random.fold_in(own, dim), (blocks,), jnp.float32, least / len(shards), top_value / len(shards)))
        gain = gain * jnp.repeat(draws, shape[dim] // blocks).reshape([-1 if axis == dim else 1 for axis in range(len(shape))])
    return gain


def bell_draw(rng, shape, width, most, split=(), held_as=jnp.bfloat16):
    values = width * jax.random.normal(rng, shape, jnp.float32)
    if split:
        values = values * level_of(rng, shape, split, -0.22, 0.18)
    return jnp.clip(values, -most, most).astype(held_as)


def setup_inputs(seed: int = 0) -> dict:
    arg_keys = jax.random.split(jax.random.key(seed), 6)
    return {
        "queries": draw_queries(jax.random.fold_in(arg_keys[5], 71), 0),
        "keys": draw_keys(jax.random.fold_in(arg_keys[5], 71), 0),
        "values": bell_draw(arg_keys[2], (NF, NH, NW, HEADS * HD), 1.0, 6.0, ((0, 8), (1, 4), (2, 8))),
        "out_grad": bell_draw(arg_keys[3], (NF, NH, NW, HEADS * HD), 1.0, 6.0, ((0, 8), (1, 4), (2, 8))),
        "extents": draw_extents(jax.random.fold_in(arg_keys[5], 71), 0),
    }


def dot_rows(left, right):
    return lax.dot_general(left, right, (((1,), (1,)), ((), ())), preferred_element_type=jnp.float32)


def dot_cols(left, right):
    return lax.dot_general(left, right, (((0,), (0,)), ((), ())), preferred_element_type=jnp.float32)


def split_heads(flat):
    count = flat.shape[0]
    return flat.reshape(count, HEADS, HD).transpose(1, 0, 2)


def merge_heads(stacked, dims):
    return stacked.transpose(1, 0, 2).reshape(tuple(dims) + (HEADS * HD,))


def positions(anchor, dims):
    result = []
    for which in range(3):
        ramp = lax.broadcasted_iota(jnp.int32, tuple(dims), which)
        result.append((anchor[which] + ramp).reshape(-1))
    return tuple(result)


def make_mask(near_pos, far_pos, reach, grid):
    keep = jnp.ones((near_pos[0].shape[0], far_pos[0].shape[0]), dtype=bool)
    for which in range(3):
        near_axis = near_pos[which]
        far_axis = far_pos[which]
        inside = (far_axis >= 0) & (far_axis < grid[which])
        keep = keep & (jnp.abs(far_axis[None, :] - near_axis[:, None]) <= reach[which]) & inside[None, :]
    return keep


def forward_tile(query_tile, key_box, anchor, extents, grid):
    tile_dims = query_tile.shape[:3]
    box_dims = key_box.shape[:3]
    chans = query_tile.shape[3]
    count = tile_dims[0] * tile_dims[1] * tile_dims[2]
    box_count = box_dims[0] * box_dims[1] * box_dims[2]
    score_scale = HD ** -0.5
    query_heads = split_heads(query_tile.reshape(count, chans))
    flat_box = key_box.reshape(box_count, 2 * chans)
    key_heads = split_heads(flat_box[:, :chans])
    value_heads = split_heads(flat_box[:, chans:])
    query_pos = positions(anchor, tile_dims)
    key_pos = positions(tuple(value - EXT for value in anchor), box_dims)

    def one_head(inputs):
        query_one, key_one, value_one, reach = inputs
        keep = make_mask(query_pos, key_pos, reach, grid)
        scores = jnp.where(keep, dot_rows(query_one, key_one) * score_scale, -1e30)
        top_score = scores.max(axis=1, keepdims=True)
        log_total = top_score + jnp.log(jnp.sum(jnp.exp(scores - top_score), axis=1, keepdims=True))
        probs = jnp.where(keep, jnp.exp(scores - log_total), 0.0)
        return jnp.dot(probs.astype(jnp.bfloat16), value_one, preferred_element_type=jnp.float32), log_total[:, 0]

    head_outs, log_totals = lax.map(one_head, (query_heads, key_heads, value_heads, extents))
    return merge_heads(head_outs, tile_dims).astype(jnp.bfloat16), log_totals.T.reshape(tuple(tile_dims) + (HEADS,))


def query_backward(query_tile, grad_tile, lse_tile, delta_tile, key_box, anchor, extents, grid):
    tile_dims = query_tile.shape[:3]
    box_dims = key_box.shape[:3]
    chans = query_tile.shape[3]
    count = tile_dims[0] * tile_dims[1] * tile_dims[2]
    box_count = box_dims[0] * box_dims[1] * box_dims[2]
    score_scale = HD ** -0.5
    query_heads = split_heads(query_tile.reshape(count, chans))
    grad_heads = split_heads(grad_tile.reshape(count, chans))
    lse_heads = lse_tile.reshape(count, HEADS).T
    delta_heads = delta_tile.reshape(count, HEADS).T
    flat_box = key_box.reshape(box_count, 2 * chans)
    key_heads = split_heads(flat_box[:, :chans])
    value_heads = split_heads(flat_box[:, chans:])
    query_pos = positions(anchor, tile_dims)
    key_pos = positions(tuple(value - EXT for value in anchor), box_dims)

    def one_head(inputs):
        query_one, grad_one, lse_one, delta_one, key_one, value_one, reach = inputs
        keep = make_mask(query_pos, key_pos, reach, grid)
        scores = dot_rows(query_one, key_one) * score_scale
        probs = jnp.where(keep, jnp.exp(scores - lse_one[:, None]), 0.0)
        dprobs = dot_rows(grad_one, value_one)
        dscores = (probs * (dprobs - delta_one[:, None]) * score_scale).astype(jnp.bfloat16)
        return jnp.dot(dscores, key_one, preferred_element_type=jnp.float32)

    grads = lax.map(one_head, (query_heads, grad_heads, lse_heads, delta_heads, key_heads, value_heads, extents))
    return merge_heads(grads, tile_dims).astype(jnp.bfloat16)


def owner_tile(own_kv, query_box, stat_box, anchor, extents, grid):
    tile_dims = own_kv.shape[:3]
    box_dims = query_box.shape[:3]
    chans = own_kv.shape[3] // 2
    count = tile_dims[0] * tile_dims[1] * tile_dims[2]
    box_count = box_dims[0] * box_dims[1] * box_dims[2]
    score_scale = HD ** -0.5
    flat_own = own_kv.reshape(count, 2 * chans)
    key_heads = split_heads(flat_own[:, :chans])
    value_heads = split_heads(flat_own[:, chans:])
    flat_box = query_box.reshape(box_count, 2 * chans)
    query_heads = split_heads(flat_box[:, :chans])
    grad_heads = split_heads(flat_box[:, chans:])
    flat_stats = stat_box.reshape(box_count, 2 * HEADS)
    lse_heads = flat_stats[:, :HEADS].T
    delta_heads = flat_stats[:, HEADS:].T
    key_pos = positions(anchor, tile_dims)
    query_pos = positions(tuple(value - EXT for value in anchor), box_dims)

    def one_head(inputs):
        key_one, value_one, query_one, grad_one, lse_one, delta_one, reach = inputs
        keep = make_mask(key_pos, query_pos, reach, grid)
        scores = dot_rows(key_one, query_one) * score_scale
        probs = jnp.where(keep, jnp.exp(scores - lse_one[None, :]), 0.0)
        dprobs = dot_rows(value_one, grad_one)
        dscores = (probs * (dprobs - delta_one[None, :]) * score_scale).astype(jnp.bfloat16)
        key_part = jnp.dot(dscores, query_one, preferred_element_type=jnp.float32)
        value_part = jnp.dot(probs.astype(jnp.bfloat16), grad_one, preferred_element_type=jnp.float32)
        return key_part, value_part

    key_parts, value_parts = lax.map(one_head, (key_heads, value_heads, query_heads, grad_heads, lse_heads, delta_heads, extents))
    return merge_heads(key_parts, tile_dims).astype(jnp.bfloat16), merge_heads(value_parts, tile_dims).astype(jnp.bfloat16)


def row_products(out_grad, attended):
    joined = out_grad.astype(jnp.float32) * attended.astype(jnp.float32)
    return joined.reshape(joined.shape[:3] + (HEADS, HD)).sum(axis=-1)


def reference(queries, keys, values, out_grad, extents):
    grid = (NF, NH, NW)
    tile_dims = (FT, HT, WT)
    box_dims = (FT + 2 * EXT, HT + 2 * EXT, WT + 2 * EXT)
    tile_total = N_FRAME * N_HEIGHT * N_WIDTH

    def pad_grid(array):
        return jnp.pad(array, ((EXT, EXT), (EXT, EXT), (EXT, EXT), (0, 0)))

    def anchor_of(index):
        frame_tile = index // (N_HEIGHT * N_WIDTH)
        row_tile = (index // N_WIDTH) % N_HEIGHT
        col_tile = index % N_WIDTH
        return (frame_tile * FT, row_tile * HT, col_tile * WT)

    def cut(array, anchor, dims):
        start = (anchor[0], anchor[1], anchor[2], jnp.int32(0))
        return lax.dynamic_slice(array, start, tuple(dims) + (array.shape[3],))

    def assemble(tiles):
        chans = tiles.shape[-1]
        grouped = tiles.reshape(N_FRAME, N_HEIGHT, N_WIDTH, FT, HT, WT, chans)
        return grouped.transpose(0, 3, 1, 4, 2, 5, 6).reshape(NF, NH, NW, chans)

    joined_kv = jnp.concatenate([keys, values], axis=-1)
    padded_kv = pad_grid(joined_kv)
    indices = jnp.arange(tile_total, dtype=jnp.int32)

    def forward_one(index):
        anchor = anchor_of(index)
        return forward_tile(cut(queries, anchor, tile_dims), cut(padded_kv, anchor, box_dims), anchor, extents, grid)

    out_tiles, lse_tiles = lax.map(forward_one, indices)
    attended = assemble(out_tiles)
    lse = assemble(lse_tiles)
    delta = row_products(out_grad, attended)
    padded_qd = pad_grid(jnp.concatenate([queries, out_grad], axis=-1))
    padded_stats = pad_grid(jnp.concatenate([lse, delta], axis=-1))

    def backward_one(index):
        anchor = anchor_of(index)
        query_part = query_backward(cut(queries, anchor, tile_dims), cut(out_grad, anchor, tile_dims),
                                    cut(lse, anchor, tile_dims), cut(delta, anchor, tile_dims),
                                    cut(padded_kv, anchor, box_dims), anchor, extents, grid)
        key_part, value_part = owner_tile(cut(joined_kv, anchor, tile_dims), cut(padded_qd, anchor, box_dims),
                                          cut(padded_stats, anchor, box_dims), anchor, extents, grid)
        return query_part, key_part, value_part

    query_tiles, key_tiles, value_tiles = lax.map(backward_one, indices)
    return attended, assemble(query_tiles), assemble(key_tiles), assemble(value_tiles)
```

```python
import functools

import jax
import jax.numpy as jnp
import numpy as np
from jax import lax
from jax.experimental import pallas as pl
from jax.experimental.pallas import tpu as pltpu
from jax.sharding import PartitionSpec as P

HEADS = 12
HD = 128
EXT = 2
TILE = (4, 6, 6)
CELLS = 144
GROUP = 2
CHUNKS = HEADS // GROUP
HALF = GROUP * HD
LANES = 2 * HALF
SCALE = HD**-0.5
LOG2E = 1.4426950408889634
MESH = pl.DeviceIdType.MESH

FP, FN, HP, HN, WP, WN, PAD, BOX = 144, 224, 304, 400, 496, 672, 848, 896
LAG = (0, 1, 2, 3, 4, 5, 6, 7, 8)
RIM, PIECE, DIRECT = 72, 144, 80
TO_NEXT = ((96, 48, WP), (FP + 48, 32, WP + 48), (FN + 48, 32, WP + 80), (HP + 64, 32, WP + 112), (HN + 64, 32, WP + 144))
TO_PREV = ((0, 48, WN), (FP, 32, WN + 48), (FN, 32, WN + 80), (HP, 32, WN + 112), (HN, 32, WN + 144))


def cell_rows():
    own = [(f, h, w) for w in range(6) for h in range(6) for f in range(4)]
    none = [(99, 99, 99)]
    fp = [(f, h, w) for w in range(6) for h in range(6) for f in (-2, -1)] + none * 8
    fn = [(f, h, w) for w in range(6) for h in range(6) for f in (4, 5)] + none * 8
    hp = [(f, h, w) for w in range(6) for h in (-2, -1) for f in range(-2, 6)]
    hn = [(f, h, w) for w in range(6) for h in (6, 7) for f in range(-2, 6)]
    rows = own + fp + fn + hp + hn
    wp = [(f, h, w - 6) if w in (4, 5) else none[0] for s, n, _ in TO_NEXT for f, h, w in rows[s : s + n]]
    wn = [(f, h, w + 6) if w in (0, 1) else none[0] for s, n, _ in TO_PREV for f, h, w in rows[s : s + n]]
    rows = rows + wp + wn + none * (BOX - PAD)
    return np.array(rows, np.int32)


def tables():
    rows = cell_rows()
    where = {tuple(cell): i for i, cell in enumerate(rows[:HP].tolist()) if cell[0] != 99}
    raw = [(f, h, w) for h in range(6) for w in range(6) for f in range(4)]
    raw_at = {cell: i for i, cell in enumerate(raw)}
    first = np.zeros((CELLS, CELLS), np.float32)
    for i, cell in enumerate(rows[:CELLS].tolist()):
        first[i, raw_at[tuple(cell)]] = 1
    rims = np.zeros((2 * RIM, CELLS), np.float32)
    for i, (f, h, w) in enumerate(rows[FN : FN + RIM].tolist()):
        rims[i, raw_at[(f - 4, h, w)]] = 1
    for i, (f, h, w) in enumerate(rows[FP : FP + RIM].tolist()):
        rims[RIM + i, raw_at[(f + 4, h, w)]] = 1
    packed = np.zeros((2 * PIECE, 2 * CELLS), np.float32)
    for s in range(2):
        packed[s * PIECE : s * PIECE + RIM, :CELLS] = rims[s * RIM : s * RIM + RIM]
        packed[s * PIECE + RIM : s * PIECE + PIECE, CELLS:] = rims[s * RIM : s * RIM + RIM]
    second = np.zeros((192, HP), np.float32)
    for i, (f, h, w) in enumerate(rows[HN : HN + 96].tolist()):
        second[i, where[(f, h - 6, w)]] = 1
    for i, (f, h, w) in enumerate(rows[HP : HP + 96].tolist()):
        second[96 + i, where[(f, h + 6, w)]] = 1
    code = np.full((CELLS, BOX), 255, np.int32)
    for axis, (one, two) in enumerate(((0x0F, 0xF0), (0x33, 0xCC), (0x55, 0xAA))):
        gap = np.abs(np.array(raw)[:, None, axis] - rows[None, :, axis])
        code &= np.where(gap <= 1, one, 0) | np.where(gap <= 2, two, 0)
    side = np.zeros((8, BOX), np.int32)
    for axis, size in enumerate(TILE):
        side |= np.where(rows[:, axis] < 0, 1 << (2 * axis), 0)[None].astype(np.int32)
        side |= np.where(rows[:, axis] >= size, 2 << (2 * axis), 0)[None].astype(np.int32)
    frames = first @ rims.T
    as_bf16 = [array.astype(jnp.bfloat16) for array in (first, packed, second, second.T, frames, first.T)]
    return (*as_bf16, code, side)


def dot(left, right, sides=((1,), (0,))):
    return lax.dot_general(left, right, (sides, ((), ())), preferred_element_type=jnp.float32)


def kernel(
    ext,
    q_ref,
    k_ref,
    v_ref,
    d_ref,
    first_ref,
    packed_ref,
    second_ref,
    second_t_ref,
    frames_ref,
    order_ref,
    code_ref,
    side_ref,
    att_out,
    dq_out,
    dk_out,
    dv_out,
    box,
    f_send,
    f_in,
    h_send,
    w_send,
    w_back,
    h_back,
    f_back,
    w_got,
    h_got,
    f_got,
    by_way,
    acc,
    send_sem,
    recv_sem,
):
    axes = ("frame", "height", "width")
    index = [lax.axis_index(axis) for axis in axes]
    has_prev = [i > 0 for i in index]
    has_next = [i < lax.axis_size(axis) - 1 for i, axis in zip(index, axes)]
    sides = []
    for axis in range(3):
        sides.append((2 * axis, axes[axis], index[axis] - 1, has_prev[axis]))
        sides.append((2 * axis + 1, axes[axis], index[axis] + 1, has_next[axis]))

    frame, frames = index[0], lax.axis_size("frame")
    shared = frames == 8
    low_mid, high_mid = frames // 2 - 1, frames // 2
    crossing = [(frame == high_mid), (frame == low_mid)] if shared else [False, False]

    def copy(src, dst, number, number_there, axis, other, c):
        return pltpu.make_async_remote_copy(
            src_ref=src,
            dst_ref=dst,
            send_sem=send_sem.at[number, c],
            recv_sem=recv_sem.at[number_there, c],
            device_id={axis: other},
            device_id_type=MESH,
        )

    def remote(src, dst, number, s, c):
        _, axis, other, _ = sides[s]
        return copy(src, dst, number, number, axis, other, c)

    box[:, PAD:BOX, :] = jnp.zeros((CHUNKS, BOX - PAD, LANES), jnp.bfloat16)
    backs = ((h_back, h_got, 96), (w_back, w_got, 176))
    regions = ((FP, FN), (FN, HP), (HP, HN), (HN, WP), (WP, WN), (WN, PAD))
    for (number, _, _, present), (low, high) in zip(sides, regions):

        @pl.when(jnp.logical_not(present))
        def _(number=number, low=low, high=high):
            if number < 2:
                at = PIECE * number
                for got in (f_in, f_got):
                    got[:, at : at + PIECE, :] = jnp.zeros((CHUNKS, PIECE, HALF), jnp.bfloat16)
            else:
                box[:, low:high, :] = jnp.zeros((CHUNKS, high - low, LANES), jnp.bfloat16)
            if number in (2, 3):
                at = 96 * (number - 2)
                h_got[:, at : at + 96, :] = jnp.zeros((CHUNKS, 96, LANES), jnp.bfloat16)

    barrier = pltpu.get_barrier_semaphore()
    for _, axis, other, present in sides:

        @pl.when(present)
        def _(axis=axis, other=other):
            pl.semaphore_signal(barrier, inc=1, device_id={axis: other}, device_id_type=MESH)

    greeted = sum(jnp.where(present, 1, 0) for _, _, _, present in sides)
    if shared:
        for here, others in ((0, (low_mid, high_mid)), (low_mid, (0, frames - 1)), (high_mid, (0, frames - 1)), (frames - 1, (low_mid, high_mid))):

            @pl.when(frame == here)
            def _(others=others):
                for other in others:
                    pl.semaphore_signal(barrier, inc=1, device_id={"frame": other}, device_id_type=MESH)

            greeted = greeted + jnp.where(frame == here, 2, 0)
    pl.semaphore_wait(barrier, greeted)

    def frame_copies(way, s, c, act):
        src, dst = ((f_send, f_in), (f_back, f_got))[way]
        here, there, number = PIECE * s, PIECE * (1 - s), 6 * way + (s ^ 1)
        if not shared:
            act(remote(src.at[c, pl.ds(here, PIECE)], dst.at[c, pl.ds(there, PIECE)], number, s, c))
            return

        @pl.when(jnp.logical_not(crossing[s]))
        def _():
            act(remote(src.at[c, pl.ds(here, PIECE)], dst.at[c, pl.ds(there, PIECE)], number, s, c))

        @pl.when(crossing[s])
        def _():
            rest = src.at[c, pl.ds(here + DIRECT, PIECE - DIRECT)]
            act(copy(rest, by_way.at[way, c], 12 + way, 12 + way, "frame", (0, frames - 1)[s], c))
            act(remote(src.at[c, pl.ds(here, DIRECT)], dst.at[c, pl.ds(there, DIRECT)], number, s, c))

    def forward(way, c, act):
        for s, here, there in ((1, 0, low_mid), (0, frames - 1, high_mid)):

            @pl.when(frame == here)
            def _(s=s, there=there):
                dst = (f_in, f_got)[way].at[c, pl.ds(PIECE * s + DIRECT, PIECE - DIRECT)]
                act(copy(by_way.at[way, c], dst, 14 + way, 6 * way + s, "frame", there, c))

    def step_forward(way, c):
        if shared:

            @pl.when((frame == 0) | (frame == frames - 1))
            def _():
                held = by_way.at[way, c]
                copy(held, held, 12 + way, 12 + way, "frame", jnp.where(frame == 0, high_mid, low_mid), c).wait_recv()

            forward(way, c, lambda copy: copy.start())

    def frames_come(way, s, c):
        got = (f_in, f_got)[way].at[c, pl.ds(PIECE * s, PIECE)]
        remote(got, got, 6 * way + s, s, c).wait_recv()

    def height_copy(s, c):
        src = h_send.at[c, pl.ds(96 * (s - 2), 96)]
        return remote(src, box.at[c, pl.ds((HN, HP)[s - 2], 96)], s ^ 1, s, c)

    def width_copy(s, c):
        src = w_send.at[c, pl.ds(176 * (s - 4), 176)]
        return remote(src, box.at[c, pl.ds((WN, WP)[s - 4], 176)], s ^ 1, s, c)

    def back_copy(s, c):
        src, dst, rows = backs[s // 2 - 1]
        low = rows * (s % 2)
        return remote(src.at[c, pl.ds(low, rows)], dst.at[c, pl.ds(rows - low, rows)], 6 + (s ^ 1), s, c)

    def region(s, c):
        return box.at[c, pl.ds(regions[s][0], regions[s][1] - regions[s][0])]

    def come(s, c):
        remote(region(s, c), region(s, c), s, s, c).wait_recv()

    def come_back(s, c):
        _, dst, rows = backs[s // 2 - 1]
        got = dst.at[c, pl.ds(rows * (s % 2), rows)]
        remote(got, got, 6 + s, s, c).wait_recv()

    def all_sent(s, c):
        if s < 2:
            for way in (0, 1):
                frame_copies(way, s, c, lambda copy: copy.wait_send())
        else:
            remote(region(s, c), region(s, c), s ^ 1, s, c).wait_send()
            back_copy(s, c).wait_send()

    def on_sides(group, act):
        for s in group:
            pl.when(sides[s][3])(functools.partial(act, s))

    def lanes_of(c, count):
        return pl.ds(pl.multiple_of(c * count * HD, count * HD), count * HD)

    def load(ref, c, count=1):
        return ref[:, :, lanes_of(c, count)].reshape(CELLS, count * HD)

    def store(ref, c, value, count=1):
        ref[:, :, lanes_of(c, count)] = value.astype(jnp.bfloat16).reshape(CELLS // 4, 4, count * HD)

    def step_first(c):
        key, value = load(k_ref, c, GROUP), load(v_ref, c, GROUP)
        f_send[c] = dot(packed_ref[...], jnp.concatenate([key, value], axis=0)).astype(jnp.bfloat16)
        on_sides((0, 1), lambda s: frame_copies(0, s, c, lambda copy: copy.start()))
        both = jnp.concatenate([key, value], axis=1)
        box[c, 0:CELLS, :] = dot(first_ref[...], both).astype(jnp.bfloat16)

    def step_frames(c):
        on_sides((0, 1), lambda s: frames_come(0, s, c))
        got = f_in[c].astype(jnp.float32)
        pad = jnp.zeros((FN - FP - RIM, HALF), jnp.float32)
        for half in (0, 1):
            low = RIM * half
            rims = [got[low : low + RIM], pad, got[PIECE + low : PIECE + low + RIM], pad]
            box[c, FP:HP, HALF * half : HALF * half + HALF] = jnp.concatenate(rims, axis=0).astype(jnp.bfloat16)
        h_send[c] = dot(second_ref[...], box[c, 0:HP, :]).astype(jnp.bfloat16)
        on_sides((2, 3), lambda s: height_copy(s, c).start())

    def step_rows(c):
        on_sides((2, 3), lambda s: come(s, c))
        for s in (4, 5):
            for start, count, there in (TO_PREV, TO_NEXT)[s - 4]:
                at = there - (WN, WP)[s - 4] + 176 * (s - 4)
                w_send[c, at : at + count, :] = box[c, start : start + count, :]
        on_sides((4, 5), lambda s: width_copy(s, c).start())

    def step_attend(c):
        on_sides((4, 5), lambda s: come(s, c))
        edges = sum(jnp.where(present, 0, 1 << number) for number, _, _, present in sides)
        open_side = (side_ref[0:1, :] & edges) == 0
        for g in range(GROUP):
            head = c * GROUP + g
            key_lanes = slice(g * HD, g * HD + HD)
            value_lanes = slice(HALF + g * HD, HALF + g * HD + HD)
            kind = (15 * ext[0, head] - 14) * (3 * ext[1, head] - 2) * ext[2, head]
            kinds = jnp.where(open_side, kind, 0)
            query, grad = load(q_ref, head), load(d_ref, head)
            key, value = box[c, :, key_lanes], box[c, :, value_lanes]
            scores = dot(query, key, ((1,), (1,)))
            scores = jnp.where((code_ref[...] & kinds) != 0, scores, -1e30)
            top = jnp.max(scores, axis=1, keepdims=True)
            raised = jnp.exp2((scores - top) * (SCALE * LOG2E))
            probs = raised * (1.0 / jnp.sum(raised, axis=1, keepdims=True))
            weights = probs.astype(jnp.bfloat16)
            attended = dot(weights, value).astype(jnp.bfloat16)
            store(att_out, head, attended)
            delta = jnp.sum(grad.astype(jnp.float32) * attended.astype(jnp.float32), axis=1, keepdims=True)
            dprobs = dot(grad, value, ((1,), (1,)))
            dscores = (probs * (dprobs - delta) * SCALE).astype(jnp.bfloat16)
            store(dq_out, head, dot(dscores, key))
            key_part = dot(dscores, query, ((0,), (0,)))
            value_part = dot(weights, grad, ((0,), (0,)))
            for part, lanes in ((key_part, key_lanes), (value_part, value_lanes)):
                acc[c, :, lanes] = part[0:WP]
                w_back[c, :, lanes] = part[WP:PAD].astype(jnp.bfloat16)
        on_sides((4, 5), lambda s: back_copy(s, c).start())

    def step_back_columns(c):
        def take(s):
            come_back(s, c)
            for start, count, there in (TO_PREV, TO_NEXT)[s - 4]:
                low = there - (WN, WP)[s - 4] + 176 * (s - 4)
                acc[c, start : start + count, :] += w_got[c, low : low + count, :].astype(jnp.float32)

        on_sides((4, 5), take)
        h_back[c] = acc[c, HP:WP, :].astype(jnp.bfloat16)
        on_sides((2, 3), lambda s: back_copy(s, c).start())

    def step_back_rows(c):
        on_sides((2, 3), lambda s: come_back(s, c))
        acc[c, 0:HP, :] += dot(second_t_ref[...], h_got[c])
        rims = [acc[c, low : low + RIM, HALF * half : HALF * half + HALF] for low in (FP, FN) for half in (0, 1)]
        f_back[c] = jnp.concatenate(rims, axis=0).astype(jnp.bfloat16)
        on_sides((0, 1), lambda s: frame_copies(1, s, c, lambda copy: copy.start()))

    def step_back_frames(c):
        on_sides((0, 1), lambda s: frames_come(1, s, c))
        got = f_got[c].astype(jnp.float32)
        halves = [jnp.concatenate([got[low : low + RIM], got[PIECE + low : PIECE + low + RIM]], axis=0) for low in (0, RIM)]
        terms = jnp.concatenate(halves, axis=1).astype(jnp.bfloat16)
        total = (acc[c, 0:CELLS, :] + dot(frames_ref[...], terms)).astype(jnp.bfloat16)
        total = dot(order_ref[...], total)
        store(dk_out, c, total[:, 0:HALF], GROUP)
        store(dv_out, c, total[:, HALF:LANES], GROUP)

    def tick(t, carry):
        for step, lag in zip(
            (
                step_first,
                functools.partial(step_forward, 0),
                step_frames,
                step_rows,
                step_attend,
                step_back_columns,
                step_back_rows,
                functools.partial(step_forward, 1),
                step_back_frames,
            ),
            LAG,
        ):
            c = t - lag
            pl.when((c >= 0) & (c < CHUNKS))(functools.partial(step, c))
        return carry

    lax.fori_loop(0, CHUNKS + LAG[-1], tick, 0)

    def finish(c, carry):
        on_sides(range(6), lambda s: all_sent(s, c))
        if shared:
            for way in (0, 1):
                forward(way, c, lambda copy: copy.wait_send())
        return carry

    lax.fori_loop(0, CHUNKS, finish, 0)


def hand_out(*refs):
    for i in range(4):
        refs[4 + i][...] = refs[i][...]


def on_device(queries, keys, values, out_grad, extents):
    flat = [array.transpose(1, 2, 0, 3).reshape(36, 4, HEADS * HD) for array in (queries, keys, values, out_grad)]
    shape = jax.ShapeDtypeStruct((36, 4, HEADS * HD), jnp.bfloat16)
    vmem = pl.BlockSpec(memory_space=pltpu.VMEM)
    wide, narrow = LANES, HALF
    held = [(BOX, wide), (288, narrow), (288, narrow), (192, wide), (352, wide), (352, wide), (192, wide), (288, narrow)]
    held += [(352, wide), (192, wide), (288, narrow)]
    results = pl.pallas_call(
        kernel,
        out_shape=(shape,) * 4,
        in_specs=[pl.BlockSpec(memory_space=pltpu.SMEM)] + [vmem] * 12,
        out_specs=(vmem,) * 4,
        scratch_shapes=[pltpu.VMEM((CHUNKS, *dims), jnp.bfloat16) for dims in held]
        + [
            pltpu.VMEM((2, CHUNKS, PIECE - DIRECT, HALF), jnp.bfloat16),
            pltpu.VMEM((CHUNKS, WP, LANES), jnp.float32),
            pltpu.SemaphoreType.DMA((16, CHUNKS)),
            pltpu.SemaphoreType.DMA((14, CHUNKS)),
        ],
        compiler_params=pltpu.CompilerParams(
            collective_id=0, has_side_effects=True, vmem_limit_bytes=42 * 1024 * 1024
        ),
        cost_estimate=pl.CostEstimate(flops=2_500_000_000, bytes_accessed=8_000_000, transcendentals=1_500_000),
    )(extents.T, *flat, *[jnp.asarray(table) for table in tables()])
    results = pl.pallas_call(
        hand_out,
        out_shape=(shape,) * 4,
        in_specs=[vmem] * 4,
        out_specs=(vmem,) * 4,
        cost_estimate=pl.CostEstimate(flops=0, bytes_accessed=3_600_000, transcendentals=0),
    )(*results)
    return tuple(result.reshape(6, 6, 4, HEADS * HD).transpose(2, 0, 1, 3) for result in results)


def solution(mesh):
    spec = P("frame", "height", "width", None)
    return jax.shard_map(
        on_device,
        mesh=mesh,
        in_specs=(spec, spec, spec, spec, P()),
        out_specs=(spec, spec, spec, spec),
        check_vma=False,
    )
```

```python
import functools

import jax
import jax.numpy as jnp
import numpy as np
from jax import lax
from jax.experimental import pallas as pl
from jax.experimental.pallas import tpu as pltpu
from jax.sharding import PartitionSpec as P

HEADS = 12
HD = 128
EXT = 2
TILE = (4, 6, 6)
CELLS = 144
GROUP = 2
CHUNKS = HEADS // GROUP
HALF = GROUP * HD
LANES = 2 * HALF
SCALE = HD**-0.5
LOG2E = 1.4426950408889634
MESH = pl.DeviceIdType.MESH

FP, FN, HP, HN, WP, WN, PAD, BOX = 144, 224, 304, 400, 496, 672, 848, 896
LAG = (0, 1, 2, 3, 4, 5, 6, 7, 8)
RIM, PIECE, DIRECT, RELAYED = 72, 144, 48, 32
TO_NEXT = ((96, 48, WP), (FP + 48, 32, WP + 48), (FN + 48, 32, WP + 80), (HP + 64, 32, WP + 112), (HN + 64, 32, WP + 144))
TO_PREV = ((0, 48, WN), (FP, 32, WN + 48), (FN, 32, WN + 80), (HP, 32, WN + 112), (HN, 32, WN + 144))


def cell_rows():
    own = [(f, h, w) for w in range(6) for h in range(6) for f in range(4)]
    none = [(99, 99, 99)]
    fp = [(f, h, w) for w in range(6) for h in range(6) for f in (-2, -1)] + none * 8
    fn = [(f, h, w) for w in range(6) for h in range(6) for f in (4, 5)] + none * 8
    hp = [(f, h, w) for w in range(6) for h in (-2, -1) for f in range(-2, 6)]
    hn = [(f, h, w) for w in range(6) for h in (6, 7) for f in range(-2, 6)]
    rows = own + fp + fn + hp + hn
    wp = [(f, h, w - 6) if w in (4, 5) else none[0] for s, n, _ in TO_NEXT for f, h, w in rows[s : s + n]]
    wn = [(f, h, w + 6) if w in (0, 1) else none[0] for s, n, _ in TO_PREV for f, h, w in rows[s : s + n]]
    rows = rows + wp + wn + none * (BOX - PAD)
    return np.array(rows, np.int32)


def tables():
    rows = cell_rows()
    where = {tuple(cell): i for i, cell in enumerate(rows[:HP].tolist()) if cell[0] != 99}
    rims = np.zeros((2 * RIM, CELLS), np.float32)
    for i, (f, h, w) in enumerate(rows[FN : FN + RIM].tolist()):
        rims[i, where[(f - 4, h, w)]] = 1
    for i, (f, h, w) in enumerate(rows[FP : FP + RIM].tolist()):
        rims[RIM + i, where[(f + 4, h, w)]] = 1
    packed = np.zeros((2 * PIECE, 2 * CELLS), np.float32)
    for s in range(2):
        packed[s * PIECE : s * PIECE + RIM, :CELLS] = rims[s * RIM : s * RIM + RIM]
        packed[s * PIECE + RIM : s * PIECE + PIECE, CELLS:] = rims[s * RIM : s * RIM + RIM]
    second = np.zeros((192, HP), np.float32)
    for i, (f, h, w) in enumerate(rows[HN : HN + 96].tolist()):
        second[i, where[(f, h - 6, w)]] = 1
    for i, (f, h, w) in enumerate(rows[HP : HP + 96].tolist()):
        second[96 + i, where[(f, h + 6, w)]] = 1
    code = np.full((CELLS, BOX), 255, np.int32)
    for axis, (one, two) in enumerate(((0x0F, 0xF0), (0x33, 0xCC), (0x55, 0xAA))):
        gap = np.abs(rows[:CELLS, None, axis] - rows[None, :, axis])
        code &= np.where(gap <= 1, one, 0) | np.where(gap <= 2, two, 0)
    side = np.zeros((8, BOX), np.int32)
    for axis, size in enumerate(TILE):
        side |= np.where(rows[:, axis] < 0, 1 << (2 * axis), 0)[None].astype(np.int32)
        side |= np.where(rows[:, axis] >= size, 2 << (2 * axis), 0)[None].astype(np.int32)
    as_bf16 = [array.astype(jnp.bfloat16) for array in (packed, second, second.T, rims.T)]
    return (*as_bf16, code, side)


def dot(left, right, sides=((1,), (0,))):
    return lax.dot_general(left, right, (sides, ((), ())), preferred_element_type=jnp.float32)


def kernel(
    ext,
    q_ref,
    k_ref,
    v_ref,
    d_ref,
    packed_ref,
    second_ref,
    second_t_ref,
    frames_ref,
    code_ref,
    side_ref,
    att_out,
    dq_out,
    dk_out,
    dv_out,
    box,
    f_send,
    f_in,
    h_send,
    w_send,
    w_back,
    h_back,
    f_back,
    w_got,
    h_got,
    f_got,
    by_way,
    acc,
    rows_ref,
    send_sem,
    recv_sem,
):
    axes = ("frame", "height", "width")
    index = [lax.axis_index(axis) for axis in axes]
    has_prev = [i > 0 for i in index]
    has_next = [i < lax.axis_size(axis) - 1 for i, axis in zip(index, axes)]
    sides = []
    for axis in range(3):
        sides.append((2 * axis, axes[axis], index[axis] - 1, has_prev[axis]))
        sides.append((2 * axis + 1, axes[axis], index[axis] + 1, has_next[axis]))

    frame, frames = index[0], lax.axis_size("frame")
    shared = frames == 8
    low_mid, high_mid = frames // 2 - 1, frames // 2
    crossing = [(frame == high_mid), (frame == low_mid)] if shared else [False, False]
    helpers = (range(low_mid), range(high_mid + 1, frames))

    def copy(src, dst, number, number_there, axis, other, c):
        return pltpu.make_async_remote_copy(
            src_ref=src,
            dst_ref=dst,
            send_sem=send_sem.at[number, c],
            recv_sem=recv_sem.at[number_there, c],
            device_id={axis: other},
            device_id_type=MESH,
        )

    def remote(src, dst, number, s, c):
        _, axis, other, _ = sides[s]
        return copy(src, dst, number, number, axis, other, c)

    box[:, PAD:BOX, :] = jnp.zeros((CHUNKS, BOX - PAD, LANES), jnp.bfloat16)
    backs = ((h_back, h_got, 96), (w_back, w_got, 176))
    regions = ((FP, FN), (FN, HP), (HP, HN), (HN, WP), (WP, WN), (WN, PAD))
    for (number, _, _, present), (low, high) in zip(sides, regions):

        @pl.when(jnp.logical_not(present))
        def _(number=number, low=low, high=high):
            if number < 2:
                at = PIECE * number
                for got in (f_in, f_got):
                    got[:, at : at + PIECE, :] = jnp.zeros((CHUNKS, PIECE, HALF), jnp.bfloat16)
            else:
                box[:, low:high, :] = jnp.zeros((CHUNKS, high - low, LANES), jnp.bfloat16)
            if number in (2, 3):
                at = 96 * (number - 2)
                h_got[:, at : at + 96, :] = jnp.zeros((CHUNKS, 96, LANES), jnp.bfloat16)

    barrier = pltpu.get_barrier_semaphore()
    for _, axis, other, present in sides:

        @pl.when(present)
        def _(axis=axis, other=other):
            pl.semaphore_signal(barrier, inc=1, device_id={axis: other}, device_id_type=MESH)

    greeted = sum(jnp.where(present, 1, 0) for _, _, _, present in sides)
    if shared:
        middle, rest = (low_mid, high_mid), [*helpers[0], *helpers[1]]
        for here in range(frames):
            others = [other for other in (rest if here in middle else middle) if abs(other - here) > 1]

            @pl.when(frame == here)
            def _(others=others):
                for other in others:
                    pl.semaphore_signal(barrier, inc=1, device_id={"frame": other}, device_id_type=MESH)

            greeted = greeted + jnp.where(frame == here, len(others), 0)
    pl.semaphore_wait(barrier, greeted)

    def frame_copies(way, s, c, act):
        src, dst = ((f_send, f_in), (f_back, f_got))[way]
        here, there, number = PIECE * s, PIECE * (1 - s), 6 * way + (s ^ 1)
        if not shared:
            act(remote(src.at[c, pl.ds(here, PIECE)], dst.at[c, pl.ds(there, PIECE)], number, s, c))
            return

        @pl.when(jnp.logical_not(crossing[s]))
        def _():
            act(remote(src.at[c, pl.ds(here, PIECE)], dst.at[c, pl.ds(there, PIECE)], number, s, c))

        @pl.when(crossing[s])
        def _():
            for i, helper in enumerate(helpers[s]):
                part = src.at[c, pl.ds(here + DIRECT + RELAYED * i, RELAYED)]
                act(copy(part, by_way.at[way, c], 12 + 4 * way + i, 12 + way, "frame", helper, c))
            act(remote(src.at[c, pl.ds(here, DIRECT)], dst.at[c, pl.ds(there, DIRECT)], number, s, c))

    def forward(way, c, act):
        for s, there in ((1, low_mid), (0, high_mid)):
            for i, helper in enumerate(helpers[1 - s]):

                @pl.when(frame == helper)
                def _(s=s, there=there, i=i):
                    rows = pl.ds(PIECE * s + DIRECT + RELAYED * i, RELAYED)
                    dst = (f_in, f_got)[way].at[c, rows]
                    act(copy(by_way.at[way, c], dst, 15 + 4 * way, 6 * way + s, "frame", there, c))

    def step_forward(way, c):
        if shared:

            @pl.when((frame < low_mid) | (frame > high_mid))
            def _():
                held = by_way.at[way, c]
                come_from = jnp.where(frame < low_mid, high_mid, low_mid)
                copy(held, held, 12 + way, 12 + way, "frame", come_from, c).wait_recv()

            forward(way, c, lambda copy: copy.start())

    def frames_come(way, s, c):
        got = (f_in, f_got)[way].at[c, pl.ds(PIECE * s, PIECE)]
        remote(got, got, 6 * way + s, s, c).wait_recv()

    def height_copy(s, c):
        src = h_send.at[c, pl.ds(96 * (s - 2), 96)]
        return remote(src, box.at[c, pl.ds((HN, HP)[s - 2], 96)], s ^ 1, s, c)

    def width_copy(s, c):
        src = w_send.at[c, pl.ds(176 * (s - 4), 176)]
        return remote(src, box.at[c, pl.ds((WN, WP)[s - 4], 176)], s ^ 1, s, c)

    def back_copy(s, c):
        src, dst, rows = backs[s // 2 - 1]
        low = rows * (s % 2)
        return remote(src.at[c, pl.ds(low, rows)], dst.at[c, pl.ds(rows - low, rows)], 6 + (s ^ 1), s, c)

    def region(s, c):
        return box.at[c, pl.ds(regions[s][0], regions[s][1] - regions[s][0])]

    def come(s, c):
        remote(region(s, c), region(s, c), s, s, c).wait_recv()

    def come_back(s, c):
        _, dst, rows = backs[s // 2 - 1]
        got = dst.at[c, pl.ds(rows * (s % 2), rows)]
        remote(got, got, 6 + s, s, c).wait_recv()

    def all_sent(s, c):
        if s < 2:
            for way in (0, 1):
                frame_copies(way, s, c, lambda copy: copy.wait_send())
        else:
            remote(region(s, c), region(s, c), s ^ 1, s, c).wait_send()
            back_copy(s, c).wait_send()

    def on_sides(group, act):
        for s in group:
            pl.when(sides[s][3])(functools.partial(act, s))

    def regroup(act):
        def column(w, carry):
            for h in (0, 2, 4):
                act((h * 6 + w, h * 6 + 6 + w), pl.ds(pl.multiple_of(w * 24 + 4 * h, 8), 8))
            return carry

        lax.fori_loop(0, 6, column, 0)

    def lanes_of(c):
        return pl.ds(pl.multiple_of(c * HALF, HALF), HALF)

    def load(refs, slot, c):
        def act(places, rows):
            for n, ref in enumerate(refs):
                pair = [ref[place, :, lanes_of(c)].astype(jnp.float32) for place in places]
                rows_ref[slot + n, rows, :] = jnp.concatenate(pair, axis=0)

        regroup(act)
        return [rows_ref[slot + n].astype(jnp.bfloat16) for n in range(len(refs))]

    def store(refs, slot, c):
        def act(places, rows):
            for n, ref in enumerate(refs):
                pair = rows_ref[slot + n, rows, :]
                for k, place in enumerate(places):
                    ref[place, :, lanes_of(c)] = pair[4 * k : 4 * k + 4].astype(jnp.bfloat16)

        regroup(act)

    def step_first(c):
        key, value = load((k_ref, v_ref), 0, c)
        f_send[c] = dot(packed_ref[...], jnp.concatenate([key, value], axis=0)).astype(jnp.bfloat16)
        on_sides((0, 1), lambda s: frame_copies(0, s, c, lambda copy: copy.start()))
        box[c, 0:CELLS, 0:HALF] = key
        box[c, 0:CELLS, HALF:LANES] = value

    def step_frames(c):
        on_sides((0, 1), lambda s: frames_come(0, s, c))
        got = f_in[c].astype(jnp.float32)
        pad = jnp.zeros((FN - FP - RIM, HALF), jnp.float32)
        for half in (0, 1):
            low = RIM * half
            rims = [got[low : low + RIM], pad, got[PIECE + low : PIECE + low + RIM], pad]
            box[c, FP:HP, HALF * half : HALF * half + HALF] = jnp.concatenate(rims, axis=0).astype(jnp.bfloat16)
        h_send[c] = dot(second_ref[...], box[c, 0:HP, :]).astype(jnp.bfloat16)
        on_sides((2, 3), lambda s: height_copy(s, c).start())

    def step_rows(c):
        on_sides((2, 3), lambda s: come(s, c))
        for s in (4, 5):
            for start, count, there in (TO_PREV, TO_NEXT)[s - 4]:
                at = there - (WN, WP)[s - 4] + 176 * (s - 4)
                w_send[c, at : at + count, :] = box[c, start : start + count, :]
        on_sides((4, 5), lambda s: width_copy(s, c).start())

    def step_attend(c):
        on_sides((4, 5), lambda s: come(s, c))
        edges = sum(jnp.where(present, 0, 1 << number) for number, _, _, present in sides)
        open_side = (side_ref[0:1, :] & edges) == 0
        queries, grads = load((q_ref, d_ref), 2, c)
        for g in range(GROUP):
            head = c * GROUP + g
            key_lanes = slice(g * HD, g * HD + HD)
            value_lanes = slice(HALF + g * HD, HALF + g * HD + HD)
            kind = (15 * ext[0, head] - 14) * (3 * ext[1, head] - 2) * ext[2, head]
            kinds = jnp.where(open_side, kind, 0)
            query, grad = queries[:, key_lanes], grads[:, key_lanes]
            key, value = box[c, :, key_lanes], box[c, :, value_lanes]
            scores = dot(query, key, ((1,), (1,)))
            scores = jnp.where((code_ref[...] & kinds) != 0, scores, -1e30)
            top = jnp.max(scores, axis=1, keepdims=True)
            raised = jnp.exp2((scores - top) * (SCALE * LOG2E))
            probs = raised * (1.0 / jnp.sum(raised, axis=1, keepdims=True))
            weights = probs.astype(jnp.bfloat16)
            attended = dot(weights, value).astype(jnp.bfloat16)
            rows_ref[4, :, key_lanes] = attended.astype(jnp.float32)
            delta = jnp.sum(grad.astype(jnp.float32) * attended.astype(jnp.float32), axis=1, keepdims=True)
            dprobs = dot(grad, value, ((1,), (1,)))
            dscores = (probs * (dprobs - delta) * SCALE).astype(jnp.bfloat16)
            rows_ref[5, :, key_lanes] = dot(dscores, key)
            key_part = dot(dscores, query, ((0,), (0,)))
            value_part = dot(weights, grad, ((0,), (0,)))
            for part, lanes in ((key_part, key_lanes), (value_part, value_lanes)):
                acc[c, :, lanes] = part[0:WP]
                w_back[c, :, lanes] = part[WP:PAD].astype(jnp.bfloat16)
        on_sides((4, 5), lambda s: back_copy(s, c).start())
        store((att_out, dq_out), 4, c)

    def step_back_columns(c):
        def take(s):
            come_back(s, c)
            for start, count, there in (TO_PREV, TO_NEXT)[s - 4]:
                low = there - (WN, WP)[s - 4] + 176 * (s - 4)
                acc[c, start : start + count, :] += w_got[c, low : low + count, :].astype(jnp.float32)

        on_sides((4, 5), take)
        h_back[c] = acc[c, HP:WP, :].astype(jnp.bfloat16)
        on_sides((2, 3), lambda s: back_copy(s, c).start())

    def step_back_rows(c):
        on_sides((2, 3), lambda s: come_back(s, c))
        acc[c, 0:HP, :] += dot(second_t_ref[...], h_got[c])
        rims = [acc[c, low : low + RIM, HALF * half : HALF * half + HALF] for low in (FP, FN) for half in (0, 1)]
        f_back[c] = jnp.concatenate(rims, axis=0).astype(jnp.bfloat16)
        on_sides((0, 1), lambda s: frame_copies(1, s, c, lambda copy: copy.start()))

    def step_back_frames(c):
        on_sides((0, 1), lambda s: frames_come(1, s, c))
        got = f_got[c].astype(jnp.float32)
        halves = [jnp.concatenate([got[low : low + RIM], got[PIECE + low : PIECE + low + RIM]], axis=0) for low in (0, RIM)]
        terms = jnp.concatenate(halves, axis=1).astype(jnp.bfloat16)
        total = acc[c, 0:CELLS, :] + dot(frames_ref[...], terms)
        rows_ref[6] = total[:, 0:HALF]
        rows_ref[7] = total[:, HALF:LANES]
        store((dk_out, dv_out), 6, c)

    def tick(t, carry):
        for step, lag in zip(
            (
                step_first,
                functools.partial(step_forward, 0),
                step_frames,
                step_rows,
                step_attend,
                step_back_columns,
                step_back_rows,
                functools.partial(step_forward, 1),
                step_back_frames,
            ),
            LAG,
        ):
            c = t - lag
            pl.when((c >= 0) & (c < CHUNKS))(functools.partial(step, c))
        return carry

    lax.fori_loop(0, CHUNKS + LAG[-1], tick, 0)

    def finish(c, carry):
        on_sides(range(6), lambda s: all_sent(s, c))
        if shared:
            for way in (0, 1):
                forward(way, c, lambda copy: copy.wait_send())
        return carry

    lax.fori_loop(0, CHUNKS, finish, 0)


def hand_out(*refs):
    for i in range(4):
        refs[4 + i][...] = refs[i][...]


def on_device(queries, keys, values, out_grad, extents):
    flat = [array.transpose(1, 2, 0, 3).reshape(36, 4, HEADS * HD) for array in (queries, keys, values, out_grad)]
    shape = jax.ShapeDtypeStruct((36, 4, HEADS * HD), jnp.bfloat16)
    vmem = pl.BlockSpec(memory_space=pltpu.VMEM)
    wide, narrow = LANES, HALF
    held = [(BOX, wide), (288, narrow), (288, narrow), (192, wide), (352, wide), (352, wide), (192, wide), (288, narrow)]
    held += [(352, wide), (192, wide), (288, narrow)]
    results = pl.pallas_call(
        kernel,
        out_shape=(shape,) * 4,
        in_specs=[pl.BlockSpec(memory_space=pltpu.SMEM)] + [vmem] * 10,
        out_specs=(vmem,) * 4,
        scratch_shapes=[pltpu.VMEM((CHUNKS, *dims), jnp.bfloat16) for dims in held]
        + [
            pltpu.VMEM((2, CHUNKS, RELAYED, HALF), jnp.bfloat16),
            pltpu.VMEM((CHUNKS, WP, LANES), jnp.float32),
            pltpu.VMEM((8, CELLS, HALF), jnp.float32),
            pltpu.SemaphoreType.DMA((20, CHUNKS)),
            pltpu.SemaphoreType.DMA((14, CHUNKS)),
        ],
        compiler_params=pltpu.CompilerParams(
            collective_id=0, has_side_effects=True, vmem_limit_bytes=60 * 1024 * 1024
        ),
        cost_estimate=pl.CostEstimate(flops=2_500_000_000, bytes_accessed=8_000_000, transcendentals=1_500_000),
    )(extents.T, *flat, *[jnp.asarray(table) for table in tables()])
    results = pl.pallas_call(
        hand_out,
        out_shape=(shape,) * 4,
        in_specs=[vmem] * 4,
        out_specs=(vmem,) * 4,
        compiler_params=pltpu.CompilerParams(vmem_limit_bytes=60 * 1024 * 1024),
        cost_estimate=pl.CostEstimate(flops=0, bytes_accessed=3_600_000, transcendentals=0),
    )(*results)
    return tuple(result.reshape(6, 6, 4, HEADS * HD).transpose(2, 0, 1, 3) for result in results)


def solution(mesh):
    spec = P("frame", "height", "width", None)
    return jax.shard_map(
        on_device,
        mesh=mesh,
        in_specs=(spec, spec, spec, spec, P()),
        out_specs=(spec, spec, spec, spec),
        check_vma=False,
    )
```

```python
import functools

import jax
import jax.numpy as jnp
import numpy as np
from jax import lax
from jax.experimental import pallas as pl
from jax.experimental.pallas import tpu as pltpu
from jax.sharding import PartitionSpec as P

HEADS = 12
HD = 128
EXT = 2
TILE = (4, 6, 6)
CELLS = 144
GROUP = 2
CHUNKS = HEADS // GROUP
HALF = GROUP * HD
LANES = 2 * HALF
SCALE = HD**-0.5
LOG2E = 1.4426950408889634
MESH = pl.DeviceIdType.MESH

FP, FN, HP, HN, WP, WN, PAD, BOX = 144, 224, 304, 400, 496, 672, 848, 896
LAG = (0, 1, 2, 3, 4, 5, 6, 7, 8)
RIM, PIECE, DIRECT, RELAYED = 72, 144, 48, 32
TO_NEXT = ((96, 48, WP), (FP + 48, 32, WP + 48), (FN + 48, 32, WP + 80), (HP + 64, 32, WP + 112), (HN + 64, 32, WP + 144))
TO_PREV = ((0, 48, WN), (FP, 32, WN + 48), (FN, 32, WN + 80), (HP, 32, WN + 112), (HN, 32, WN + 144))


def cell_rows():
    own = [(f, h, w) for w in range(6) for h in range(6) for f in range(4)]
    none = [(99, 99, 99)]
    fp = [(f, h, w) for w in range(6) for h in range(6) for f in (-2, -1)] + none * 8
    fn = [(f, h, w) for w in range(6) for h in range(6) for f in (4, 5)] + none * 8
    hp = [(f, h, w) for w in range(6) for h in (-2, -1) for f in range(-2, 6)]
    hn = [(f, h, w) for w in range(6) for h in (6, 7) for f in range(-2, 6)]
    rows = own + fp + fn + hp + hn
    wp = [(f, h, w - 6) if w in (4, 5) else none[0] for s, n, _ in TO_NEXT for f, h, w in rows[s : s + n]]
    wn = [(f, h, w + 6) if w in (0, 1) else none[0] for s, n, _ in TO_PREV for f, h, w in rows[s : s + n]]
    rows = rows + wp + wn + none * (BOX - PAD)
    return np.array(rows, np.int32)


def tables():
    rows = cell_rows()
    where = {tuple(cell): i for i, cell in enumerate(rows[:HP].tolist()) if cell[0] != 99}
    rims = np.zeros((2 * RIM, CELLS), np.float32)
    for i, (f, h, w) in enumerate(rows[FN : FN + RIM].tolist()):
        rims[i, where[(f - 4, h, w)]] = 1
    for i, (f, h, w) in enumerate(rows[FP : FP + RIM].tolist()):
        rims[RIM + i, where[(f + 4, h, w)]] = 1
    packed = np.zeros((2 * PIECE, 2 * CELLS), np.float32)
    for s in range(2):
        packed[s * PIECE : s * PIECE + RIM, :CELLS] = rims[s * RIM : s * RIM + RIM]
        packed[s * PIECE + RIM : s * PIECE + PIECE, CELLS:] = rims[s * RIM : s * RIM + RIM]
    second = np.zeros((192, HP), np.float32)
    for i, (f, h, w) in enumerate(rows[HN : HN + 96].tolist()):
        second[i, where[(f, h - 6, w)]] = 1
    for i, (f, h, w) in enumerate(rows[HP : HP + 96].tolist()):
        second[96 + i, where[(f, h + 6, w)]] = 1
    code = np.full((CELLS, BOX), 255, np.int32)
    for axis, (one, two) in enumerate(((0x0F, 0xF0), (0x33, 0xCC), (0x55, 0xAA))):
        gap = np.abs(rows[:CELLS, None, axis] - rows[None, :, axis])
        code &= np.where(gap <= 1, one, 0) | np.where(gap <= 2, two, 0)
    side = np.zeros((8, BOX), np.int32)
    for axis, size in enumerate(TILE):
        side |= np.where(rows[:, axis] < 0, 1 << (2 * axis), 0)[None].astype(np.int32)
        side |= np.where(rows[:, axis] >= size, 2 << (2 * axis), 0)[None].astype(np.int32)
    as_bf16 = [array.astype(jnp.bfloat16) for array in (packed, second, second.T, rims.T)]
    return (*as_bf16, code, side)


def dot(left, right, sides=((1,), (0,))):
    return lax.dot_general(left, right, (sides, ((), ())), preferred_element_type=jnp.float32)


def kernel(
    ext,
    q_ref,
    k_ref,
    v_ref,
    d_ref,
    packed_ref,
    second_ref,
    second_t_ref,
    frames_ref,
    code_ref,
    side_ref,
    att_out,
    dq_out,
    dk_out,
    dv_out,
    box,
    f_send,
    f_in,
    h_send,
    w_send,
    w_back,
    h_back,
    f_back,
    w_got,
    h_got,
    f_got,
    by_way,
    acc,
    rows_ref,
    send_sem,
    recv_sem,
):
    axes = ("frame", "height", "width")
    index = [lax.axis_index(axis) for axis in axes]
    has_prev = [i > 0 for i in index]
    has_next = [i < lax.axis_size(axis) - 1 for i, axis in zip(index, axes)]
    sides = []
    for axis in range(3):
        sides.append((2 * axis, axes[axis], index[axis] - 1, has_prev[axis]))
        sides.append((2 * axis + 1, axes[axis], index[axis] + 1, has_next[axis]))

    frame, frames = index[0], lax.axis_size("frame")
    shared = frames == 8
    low_mid, high_mid = frames // 2 - 1, frames // 2
    crossing = [(frame == high_mid), (frame == low_mid)] if shared else [False, False]
    helpers = (range(low_mid), range(high_mid + 1, frames))

    def copy(src, dst, number, number_there, axis, other, c):
        return pltpu.make_async_remote_copy(
            src_ref=src,
            dst_ref=dst,
            send_sem=send_sem.at[number, c],
            recv_sem=recv_sem.at[number_there, c],
            device_id={axis: other},
            device_id_type=MESH,
        )

    def remote(src, dst, number, s, c):
        _, axis, other, _ = sides[s]
        return copy(src, dst, number, number, axis, other, c)

    box[:, PAD:BOX, :] = jnp.zeros((CHUNKS, BOX - PAD, LANES), jnp.bfloat16)
    backs = ((h_back, h_got, 96), (w_back, w_got, 176))
    regions = ((FP, FN), (FN, HP), (HP, HN), (HN, WP), (WP, WN), (WN, PAD))
    for (number, _, _, present), (low, high) in zip(sides, regions):

        @pl.when(jnp.logical_not(present))
        def _(number=number, low=low, high=high):
            if number < 2:
                at = PIECE * number
                for got in (f_in, f_got):
                    got[:, at : at + PIECE, :] = jnp.zeros((CHUNKS, PIECE, HALF), jnp.bfloat16)
            else:
                box[:, low:high, :] = jnp.zeros((CHUNKS, high - low, LANES), jnp.bfloat16)
            if number in (2, 3):
                at = 96 * (number - 2)
                h_got[:, at : at + 96, :] = jnp.zeros((CHUNKS, 96, LANES), jnp.bfloat16)

    barrier = pltpu.get_barrier_semaphore()
    for _, axis, other, present in sides:

        @pl.when(present)
        def _(axis=axis, other=other):
            pl.semaphore_signal(barrier, inc=1, device_id={axis: other}, device_id_type=MESH)

    greeted = sum(jnp.where(present, 1, 0) for _, _, _, present in sides)
    if shared:
        middle, rest = (low_mid, high_mid), [*helpers[0], *helpers[1]]
        for here in range(frames):
            others = [other for other in (rest if here in middle else middle) if abs(other - here) > 1]

            @pl.when(frame == here)
            def _(others=others):
                for other in others:
                    pl.semaphore_signal(barrier, inc=1, device_id={"frame": other}, device_id_type=MESH)

            greeted = greeted + jnp.where(frame == here, len(others), 0)
    pl.semaphore_wait(barrier, greeted)

    def frame_copies(way, s, c, act):
        src, dst = ((f_send, f_in), (f_back, f_got))[way]
        here, there, number = PIECE * s, PIECE * (1 - s), 6 * way + (s ^ 1)
        if not shared:
            act(remote(src.at[c, pl.ds(here, PIECE)], dst.at[c, pl.ds(there, PIECE)], number, s, c))
            return

        @pl.when(jnp.logical_not(crossing[s]))
        def _():
            act(remote(src.at[c, pl.ds(here, PIECE)], dst.at[c, pl.ds(there, PIECE)], number, s, c))

        @pl.when(crossing[s])
        def _():
            for i, helper in enumerate(helpers[1 - s]):
                part = src.at[c, pl.ds(here + DIRECT + RELAYED * i, RELAYED)]
                act(copy(part, by_way.at[way, c], 12 + 4 * way + i, 12 + way, "frame", helper, c))
            act(remote(src.at[c, pl.ds(here, DIRECT)], dst.at[c, pl.ds(there, DIRECT)], number, s, c))

    def forward(way, c, act):
        for s, there in ((1, low_mid), (0, high_mid)):
            for i, helper in enumerate(helpers[s]):

                @pl.when(frame == helper)
                def _(s=s, there=there, i=i):
                    rows = pl.ds(PIECE * s + DIRECT + RELAYED * i, RELAYED)
                    dst = (f_in, f_got)[way].at[c, rows]
                    act(copy(by_way.at[way, c], dst, 15 + 4 * way, 6 * way + s, "frame", there, c))

    def step_forward(way, c):
        if shared:

            @pl.when((frame < low_mid) | (frame > high_mid))
            def _():
                held = by_way.at[way, c]
                come_from = jnp.where(frame < low_mid, low_mid, high_mid)
                copy(held, held, 12 + way, 12 + way, "frame", come_from, c).wait_recv()

            forward(way, c, lambda copy: copy.start())

    def frames_come(way, s, c):
        got = (f_in, f_got)[way].at[c, pl.ds(PIECE * s, PIECE)]
        remote(got, got, 6 * way + s, s, c).wait_recv()

    def height_copy(s, c):
        src = h_send.at[c, pl.ds(96 * (s - 2), 96)]
        return remote(src, box.at[c, pl.ds((HN, HP)[s - 2], 96)], s ^ 1, s, c)

    def width_copy(s, c):
        src = w_send.at[c, pl.ds(176 * (s - 4), 176)]
        return remote(src, box.at[c, pl.ds((WN, WP)[s - 4], 176)], s ^ 1, s, c)

    def back_copy(s, c):
        src, dst, rows = backs[s // 2 - 1]
        low = rows * (s % 2)
        return remote(src.at[c, pl.ds(low, rows)], dst.at[c, pl.ds(rows - low, rows)], 6 + (s ^ 1), s, c)

    def region(s, c):
        return box.at[c, pl.ds(regions[s][0], regions[s][1] - regions[s][0])]

    def come(s, c):
        remote(region(s, c), region(s, c), s, s, c).wait_recv()

    def come_back(s, c):
        _, dst, rows = backs[s // 2 - 1]
        got = dst.at[c, pl.ds(rows * (s % 2), rows)]
        remote(got, got, 6 + s, s, c).wait_recv()

    def all_sent(s, c):
        if s < 2:
            for way in (0, 1):
                frame_copies(way, s, c, lambda copy: copy.wait_send())
        else:
            remote(region(s, c), region(s, c), s ^ 1, s, c).wait_send()
            back_copy(s, c).wait_send()

    def on_sides(group, act):
        for s in group:
            pl.when(sides[s][3])(functools.partial(act, s))

    def regroup(act):
        def column(w, carry):
            for h in (0, 2, 4):
                act((h * 6 + w, h * 6 + 6 + w), pl.ds(pl.multiple_of(w * 24 + 4 * h, 8), 8))
            return carry

        lax.fori_loop(0, 6, column, 0)

    def lanes_of(c):
        return pl.ds(pl.multiple_of(c * HALF, HALF), HALF)

    def load(refs, slot, c):
        def act(places, rows):
            for n, ref in enumerate(refs):
                pair = [ref[place, :, lanes_of(c)].astype(jnp.float32) for place in places]
                rows_ref[slot + n, rows, :] = jnp.concatenate(pair, axis=0)

        regroup(act)
        return [rows_ref[slot + n].astype(jnp.bfloat16) for n in range(len(refs))]

    def store(refs, slot, c):
        def act(places, rows):
            for n, ref in enumerate(refs):
                pair = rows_ref[slot + n, rows, :]
                for k, place in enumerate(places):
                    ref[place, :, lanes_of(c)] = pair[4 * k : 4 * k + 4].astype(jnp.bfloat16)

        regroup(act)

    def step_first(c):
        key, value = load((k_ref, v_ref), 0, c)
        f_send[c] = dot(packed_ref[...], jnp.concatenate([key, value], axis=0)).astype(jnp.bfloat16)
        on_sides((0, 1), lambda s: frame_copies(0, s, c, lambda copy: copy.start()))
        box[c, 0:CELLS, 0:HALF] = key
        box[c, 0:CELLS, HALF:LANES] = value

    def step_frames(c):
        on_sides((0, 1), lambda s: frames_come(0, s, c))
        got = f_in[c].astype(jnp.float32)
        pad = jnp.zeros((FN - FP - RIM, HALF), jnp.float32)
        for half in (0, 1):
            low = RIM * half
            rims = [got[low : low + RIM], pad, got[PIECE + low : PIECE + low + RIM], pad]
            box[c, FP:HP, HALF * half : HALF * half + HALF] = jnp.concatenate(rims, axis=0).astype(jnp.bfloat16)
        h_send[c] = dot(second_ref[...], box[c, 0:HP, :]).astype(jnp.bfloat16)
        on_sides((2, 3), lambda s: height_copy(s, c).start())

    def step_rows(c):
        on_sides((2, 3), lambda s: come(s, c))
        for s in (4, 5):
            for start, count, there in (TO_PREV, TO_NEXT)[s - 4]:
                at = there - (WN, WP)[s - 4] + 176 * (s - 4)
                w_send[c, at : at + count, :] = box[c, start : start + count, :]
        on_sides((4, 5), lambda s: width_copy(s, c).start())

    def step_attend(c):
        on_sides((4, 5), lambda s: come(s, c))
        edges = sum(jnp.where(present, 0, 1 << number) for number, _, _, present in sides)
        open_side = (side_ref[0:1, :] & edges) == 0
        queries, grads = load((q_ref, d_ref), 2, c)
        for g in range(GROUP):
            head = c * GROUP + g
            key_lanes = slice(g * HD, g * HD + HD)
            value_lanes = slice(HALF + g * HD, HALF + g * HD + HD)
            kind = (15 * ext[0, head] - 14) * (3 * ext[1, head] - 2) * ext[2, head]
            kinds = jnp.where(open_side, kind, 0)
            query, grad = queries[:, key_lanes], grads[:, key_lanes]
            key, value = box[c, :, key_lanes], box[c, :, value_lanes]
            scores = dot(query, key, ((1,), (1,)))
            scores = jnp.where((code_ref[...] & kinds) != 0, scores, -1e30)
            top = jnp.max(scores, axis=1, keepdims=True)
            raised = jnp.exp2((scores - top) * (SCALE * LOG2E))
            probs = raised * (1.0 / jnp.sum(raised, axis=1, keepdims=True))
            weights = probs.astype(jnp.bfloat16)
            attended = dot(weights, value).astype(jnp.bfloat16)
            rows_ref[4, :, key_lanes] = attended.astype(jnp.float32)
            delta = jnp.sum(grad.astype(jnp.float32) * attended.astype(jnp.float32), axis=1, keepdims=True)
            dprobs = dot(grad, value, ((1,), (1,)))
            dscores = (probs * (dprobs - delta) * SCALE).astype(jnp.bfloat16)
            rows_ref[5, :, key_lanes] = dot(dscores, key)
            key_part = dot(dscores, query, ((0,), (0,)))
            value_part = dot(weights, grad, ((0,), (0,)))
            for part, lanes in ((key_part, key_lanes), (value_part, value_lanes)):
                acc[c, :, lanes] = part[0:WP]
                w_back[c, :, lanes] = part[WP:PAD].astype(jnp.bfloat16)
        on_sides((4, 5), lambda s: back_copy(s, c).start())
        store((att_out, dq_out), 4, c)

    def step_back_columns(c):
        def take(s):
            come_back(s, c)
            for start, count, there in (TO_PREV, TO_NEXT)[s - 4]:
                low = there - (WN, WP)[s - 4] + 176 * (s - 4)
                acc[c, start : start + count, :] += w_got[c, low : low + count, :].astype(jnp.float32)

        on_sides((4, 5), take)
        h_back[c] = acc[c, HP:WP, :].astype(jnp.bfloat16)
        on_sides((2, 3), lambda s: back_copy(s, c).start())

    def step_back_rows(c):
        on_sides((2, 3), lambda s: come_back(s, c))
        acc[c, 0:HP, :] += dot(second_t_ref[...], h_got[c])
        rims = [acc[c, low : low + RIM, HALF * half : HALF * half + HALF] for low in (FP, FN) for half in (0, 1)]
        f_back[c] = jnp.concatenate(rims, axis=0).astype(jnp.bfloat16)
        on_sides((0, 1), lambda s: frame_copies(1, s, c, lambda copy: copy.start()))

    def step_back_frames(c):
        on_sides((0, 1), lambda s: frames_come(1, s, c))
        got = f_got[c].astype(jnp.float32)
        halves = [jnp.concatenate([got[low : low + RIM], got[PIECE + low : PIECE + low + RIM]], axis=0) for low in (0, RIM)]
        terms = jnp.concatenate(halves, axis=1).astype(jnp.bfloat16)
        total = acc[c, 0:CELLS, :] + dot(frames_ref[...], terms)
        rows_ref[6] = total[:, 0:HALF]
        rows_ref[7] = total[:, HALF:LANES]
        store((dk_out, dv_out), 6, c)

    def tick(t, carry):
        for step, lag in zip(
            (
                step_first,
                functools.partial(step_forward, 0),
                step_frames,
                step_rows,
                step_attend,
                step_back_columns,
                step_back_rows,
                functools.partial(step_forward, 1),
                step_back_frames,
            ),
            LAG,
        ):
            c = t - lag
            pl.when((c >= 0) & (c < CHUNKS))(functools.partial(step, c))
        return carry

    lax.fori_loop(0, CHUNKS + LAG[-1], tick, 0)

    def finish(c, carry):
        on_sides(range(6), lambda s: all_sent(s, c))
        if shared:
            for way in (0, 1):
                forward(way, c, lambda copy: copy.wait_send())
        return carry

    lax.fori_loop(0, CHUNKS, finish, 0)


def hand_out(*refs):
    for i in range(4):
        refs[4 + i][...] = refs[i][...]


def on_device(queries, keys, values, out_grad, extents):
    flat = [array.transpose(1, 2, 0, 3).reshape(36, 4, HEADS * HD) for array in (queries, keys, values, out_grad)]
    shape = jax.ShapeDtypeStruct((36, 4, HEADS * HD), jnp.bfloat16)
    vmem = pl.BlockSpec(memory_space=pltpu.VMEM)
    wide, narrow = LANES, HALF
    held = [(BOX, wide), (288, narrow), (288, narrow), (192, wide), (352, wide), (352, wide), (192, wide), (288, narrow)]
    held += [(352, wide), (192, wide), (288, narrow)]
    results = pl.pallas_call(
        kernel,
        out_shape=(shape,) * 4,
        in_specs=[pl.BlockSpec(memory_space=pltpu.SMEM)] + [vmem] * 10,
        out_specs=(vmem,) * 4,
        scratch_shapes=[pltpu.VMEM((CHUNKS, *dims), jnp.bfloat16) for dims in held]
        + [
            pltpu.VMEM((2, CHUNKS, RELAYED, HALF), jnp.bfloat16),
            pltpu.VMEM((CHUNKS, WP, LANES), jnp.float32),
            pltpu.VMEM((8, CELLS, HALF), jnp.float32),
            pltpu.SemaphoreType.DMA((20, CHUNKS)),
            pltpu.SemaphoreType.DMA((14, CHUNKS)),
        ],
        compiler_params=pltpu.CompilerParams(
            collective_id=0, has_side_effects=True, vmem_limit_bytes=60 * 1024 * 1024
        ),
        cost_estimate=pl.CostEstimate(flops=2_500_000_000, bytes_accessed=8_000_000, transcendentals=1_500_000),
    )(extents.T, *flat, *[jnp.asarray(table) for table in tables()])
    results = pl.pallas_call(
        hand_out,
        out_shape=(shape,) * 4,
        in_specs=[vmem] * 4,
        out_specs=(vmem,) * 4,
        compiler_params=pltpu.CompilerParams(vmem_limit_bytes=60 * 1024 * 1024),
        cost_estimate=pl.CostEstimate(flops=0, bytes_accessed=3_600_000, transcendentals=0),
    )(*results)
    return tuple(result.reshape(6, 6, 4, HEADS * HD).transpose(2, 0, 1, 3) for result in results)


def solution(mesh):
    spec = P("frame", "height", "width", None)
    return jax.shard_map(
        on_device,
        mesh=mesh,
        in_specs=(spec, spec, spec, spec, P()),
        out_specs=(spec, spec, spec, spec),
        check_vma=False,
    )
```

```python
import functools

import jax
import jax.numpy as jnp
import numpy as np
from jax import lax
from jax.experimental import pallas as pl
from jax.experimental.pallas import tpu as pltpu
from jax.sharding import PartitionSpec as P

HEADS = 12
HD = 128
EXT = 2
TILE = (4, 6, 6)
CELLS = 144
GROUP = 2
CHUNKS = HEADS // GROUP
HALF = GROUP * HD
LANES = 2 * HALF
SCALE = HD**-0.5
LOG2E = 1.4426950408889634
MESH = pl.DeviceIdType.MESH

FP, FN, HP, HN, WP, WN, PAD, BOX = 144, 224, 304, 400, 496, 672, 848, 896
LAG = (0, 1, 2, 3, 4, -1, 5, 6, 7, 8)
RIM, PIECE, DIRECT, RELAYED = 72, 144, 48, 32
TO_NEXT = ((96, 48, WP), (FP + 48, 32, WP + 48), (FN + 48, 32, WP + 80), (HP + 64, 32, WP + 112), (HN + 64, 32, WP + 144))
TO_PREV = ((0, 48, WN), (FP, 32, WN + 48), (FN, 32, WN + 80), (HP, 32, WN + 112), (HN, 32, WN + 144))


def cell_rows():
    own = [(f, h, w) for w in range(6) for h in range(6) for f in range(4)]
    none = [(99, 99, 99)]
    fp = [(f, h, w) for w in range(6) for h in range(6) for f in (-2, -1)] + none * 8
    fn = [(f, h, w) for w in range(6) for h in range(6) for f in (4, 5)] + none * 8
    hp = [(f, h, w) for w in range(6) for h in (-2, -1) for f in range(-2, 6)]
    hn = [(f, h, w) for w in range(6) for h in (6, 7) for f in range(-2, 6)]
    rows = own + fp + fn + hp + hn
    wp = [(f, h, w - 6) if w in (4, 5) else none[0] for s, n, _ in TO_NEXT for f, h, w in rows[s : s + n]]
    wn = [(f, h, w + 6) if w in (0, 1) else none[0] for s, n, _ in TO_PREV for f, h, w in rows[s : s + n]]
    rows = rows + wp + wn + none * (BOX - PAD)
    return np.array(rows, np.int32)


def tables():
    rows = cell_rows()
    where = {tuple(cell): i for i, cell in enumerate(rows[:HP].tolist()) if cell[0] != 99}
    rims = np.zeros((2 * RIM, CELLS), np.float32)
    for i, (f, h, w) in enumerate(rows[FN : FN + RIM].tolist()):
        rims[i, where[(f - 4, h, w)]] = 1
    for i, (f, h, w) in enumerate(rows[FP : FP + RIM].tolist()):
        rims[RIM + i, where[(f + 4, h, w)]] = 1
    packed = np.zeros((2 * PIECE, 2 * CELLS), np.float32)
    for s in range(2):
        packed[s * PIECE : s * PIECE + RIM, :CELLS] = rims[s * RIM : s * RIM + RIM]
        packed[s * PIECE + RIM : s * PIECE + PIECE, CELLS:] = rims[s * RIM : s * RIM + RIM]
    second = np.zeros((192, HP), np.float32)
    for i, (f, h, w) in enumerate(rows[HN : HN + 96].tolist()):
        second[i, where[(f, h - 6, w)]] = 1
    for i, (f, h, w) in enumerate(rows[HP : HP + 96].tolist()):
        second[96 + i, where[(f, h + 6, w)]] = 1
    code = np.full((CELLS, BOX), 255, np.int32)
    for axis, (one, two) in enumerate(((0x0F, 0xF0), (0x33, 0xCC), (0x55, 0xAA))):
        gap = np.abs(rows[:CELLS, None, axis] - rows[None, :, axis])
        code &= np.where(gap <= 1, one, 0) | np.where(gap <= 2, two, 0)
    side = np.zeros((8, BOX), np.int32)
    for axis, size in enumerate(TILE):
        side |= np.where(rows[:, axis] < 0, 1 << (2 * axis), 0)[None].astype(np.int32)
        side |= np.where(rows[:, axis] >= size, 2 << (2 * axis), 0)[None].astype(np.int32)
    as_bf16 = [array.astype(jnp.bfloat16) for array in (packed, second, second.T, rims.T)]
    return (*as_bf16, code, side)


def dot(left, right, sides=((1,), (0,))):
    return lax.dot_general(left, right, (sides, ((), ())), preferred_element_type=jnp.float32)


def kernel(ext, side_ref, *refs):
    (q_hbm, k_hbm, v_hbm, d_hbm, packed_hbm, second_hbm, second_t_hbm, frames_hbm, code_hbm) = refs[:9]
    outs = refs[9:13]
    (q_ref, k_ref, v_ref, d_ref, packed_ref, second_ref, second_t_ref, frames_ref, code_ref) = refs[13:22]
    att_out, dq_out, dk_out, dv_out = results = refs[22:26]
    (box, f_send, f_in, h_send, w_send, w_back, h_back, f_back, w_got, h_got, f_got, by_way, acc, rows_ref) = refs[26:40]
    send_sem, recv_sem, in_sem, out_sem = refs[40:]

    load_first = ((k_hbm, k_ref), (v_hbm, v_ref), (packed_hbm, packed_ref))
    load_frames = ((second_hbm, second_ref),)
    load_attend = ((q_hbm, q_ref), (d_hbm, d_ref), (code_hbm, code_ref))
    load_back = ((second_t_hbm, second_t_ref), (frames_hbm, frames_ref))
    loads = (*load_first, *load_frames, *load_attend, *load_back)

    def operand(pair):
        number = [other[1] is pair[1] for other in loads].index(True)
        return pltpu.make_async_copy(*pair, in_sem.at[number])

    for pair in loads:
        operand(pair).start()

    def arrive(pairs):
        for pair in pairs:
            operand(pair).wait()

    def leave(number, c):
        if number < 2:
            return pltpu.make_async_copy(results[number], outs[number], out_sem.at[number, 0])
        lanes = pl.ds(pl.multiple_of(c * HALF, HALF), HALF)
        return pltpu.make_async_copy(results[number].at[:, :, lanes], outs[number].at[:, :, lanes], out_sem.at[number, c])

    axes = ("frame", "height", "width")
    index = [lax.axis_index(axis) for axis in axes]
    has_prev = [i > 0 for i in index]
    has_next = [i < lax.axis_size(axis) - 1 for i, axis in zip(index, axes)]
    sides = []
    for axis in range(3):
        sides.append((2 * axis, axes[axis], index[axis] - 1, has_prev[axis]))
        sides.append((2 * axis + 1, axes[axis], index[axis] + 1, has_next[axis]))

    frame, frames = index[0], lax.axis_size("frame")
    shared = frames == 8
    low_mid, high_mid = frames // 2 - 1, frames // 2
    crossing = [(frame == high_mid), (frame == low_mid)] if shared else [False, False]
    helpers = (range(low_mid), range(high_mid + 1, frames))

    def copy(src, dst, number, number_there, axis, other, c):
        return pltpu.make_async_remote_copy(
            src_ref=src,
            dst_ref=dst,
            send_sem=send_sem.at[number, c],
            recv_sem=recv_sem.at[number_there, c],
            device_id={axis: other},
            device_id_type=MESH,
        )

    def remote(src, dst, number, s, c):
        _, axis, other, _ = sides[s]
        return copy(src, dst, number, number, axis, other, c)

    box[:, PAD:BOX, :] = jnp.zeros((CHUNKS, BOX - PAD, LANES), jnp.bfloat16)
    backs = ((h_back, h_got, 96), (w_back, w_got, 176))
    regions = ((FP, FN), (FN, HP), (HP, HN), (HN, WP), (WP, WN), (WN, PAD))
    for (number, _, _, present), (low, high) in zip(sides, regions):

        @pl.when(jnp.logical_not(present))
        def _(number=number, low=low, high=high):
            if number < 2:
                at = PIECE * number
                for got in (f_in, f_got):
                    got[:, at : at + PIECE, :] = jnp.zeros((CHUNKS, PIECE, HALF), jnp.bfloat16)
            else:
                box[:, low:high, :] = jnp.zeros((CHUNKS, high - low, LANES), jnp.bfloat16)
            if number in (2, 3):
                at = 96 * (number - 2)
                h_got[:, at : at + 96, :] = jnp.zeros((CHUNKS, 96, LANES), jnp.bfloat16)

    barrier = pltpu.get_barrier_semaphore()
    for _, axis, other, present in sides:

        @pl.when(present)
        def _(axis=axis, other=other):
            pl.semaphore_signal(barrier, inc=1, device_id={axis: other}, device_id_type=MESH)

    greeted = sum(jnp.where(present, 1, 0) for _, _, _, present in sides)
    if shared:
        middle, rest = (low_mid, high_mid), [*helpers[0], *helpers[1]]
        for here in range(frames):
            others = [other for other in (rest if here in middle else middle) if abs(other - here) > 1]

            @pl.when(frame == here)
            def _(others=others):
                for other in others:
                    pl.semaphore_signal(barrier, inc=1, device_id={"frame": other}, device_id_type=MESH)

            greeted = greeted + jnp.where(frame == here, len(others), 0)
    def frame_copies(way, s, c, act):
        src, dst = ((f_send, f_in), (f_back, f_got))[way]
        here, there, number = PIECE * s, PIECE * (1 - s), 6 * way + (s ^ 1)
        if not shared:
            act(remote(src.at[c, pl.ds(here, PIECE)], dst.at[c, pl.ds(there, PIECE)], number, s, c))
            return

        @pl.when(jnp.logical_not(crossing[s]))
        def _():
            act(remote(src.at[c, pl.ds(here, PIECE)], dst.at[c, pl.ds(there, PIECE)], number, s, c))

        @pl.when(crossing[s])
        def _():
            for i, helper in enumerate(helpers[1 - s]):
                part = src.at[c, pl.ds(here + DIRECT + RELAYED * i, RELAYED)]
                act(copy(part, by_way.at[way, c], 12 + 4 * way + i, 12 + way, "frame", helper, c))
            act(remote(src.at[c, pl.ds(here, DIRECT)], dst.at[c, pl.ds(there, DIRECT)], number, s, c))

    def forward(way, c, act):
        for s, there in ((1, low_mid), (0, high_mid)):
            for i, helper in enumerate(helpers[s]):

                @pl.when(frame == helper)
                def _(s=s, there=there, i=i):
                    rows = pl.ds(PIECE * s + DIRECT + RELAYED * i, RELAYED)
                    dst = (f_in, f_got)[way].at[c, rows]
                    act(copy(by_way.at[way, c], dst, 15 + 4 * way, 6 * way + s, "frame", there, c))

    def step_forward(way, c):
        if shared:

            @pl.when((frame < low_mid) | (frame > high_mid))
            def _():
                held = by_way.at[way, c]
                come_from = jnp.where(frame < low_mid, low_mid, high_mid)
                copy(held, held, 12 + way, 12 + way, "frame", come_from, c).wait_recv()

            forward(way, c, lambda copy: copy.start())

    def frames_come(way, s, c):
        got = (f_in, f_got)[way].at[c, pl.ds(PIECE * s, PIECE)]
        remote(got, got, 6 * way + s, s, c).wait_recv()

    def height_copy(s, c):
        src = h_send.at[c, pl.ds(96 * (s - 2), 96)]
        return remote(src, box.at[c, pl.ds((HN, HP)[s - 2], 96)], s ^ 1, s, c)

    def width_copy(s, c):
        src = w_send.at[c, pl.ds(176 * (s - 4), 176)]
        return remote(src, box.at[c, pl.ds((WN, WP)[s - 4], 176)], s ^ 1, s, c)

    def back_copy(s, c):
        src, dst, rows = backs[s // 2 - 1]
        low = rows * (s % 2)
        return remote(src.at[c, pl.ds(low, rows)], dst.at[c, pl.ds(rows - low, rows)], 6 + (s ^ 1), s, c)

    def region(s, c):
        return box.at[c, pl.ds(regions[s][0], regions[s][1] - regions[s][0])]

    def come(s, c):
        remote(region(s, c), region(s, c), s, s, c).wait_recv()

    def come_back(s, c):
        _, dst, rows = backs[s // 2 - 1]
        got = dst.at[c, pl.ds(rows * (s % 2), rows)]
        remote(got, got, 6 + s, s, c).wait_recv()

    def all_sent(s, c):
        if s < 2:
            for way in (0, 1):
                frame_copies(way, s, c, lambda copy: copy.wait_send())
        else:
            remote(region(s, c), region(s, c), s ^ 1, s, c).wait_send()
            back_copy(s, c).wait_send()

    def on_sides(group, act):
        for s in group:
            pl.when(sides[s][3])(functools.partial(act, s))

    def regroup(act):
        def column(w, carry):
            for h in (0, 2, 4):
                act((h * 6 + w, h * 6 + 6 + w), pl.ds(pl.multiple_of(w * 24 + 4 * h, 8), 8))
            return carry

        lax.fori_loop(0, 6, column, 0)

    def lanes_of(c):
        return pl.ds(pl.multiple_of(c * HALF, HALF), HALF)

    def load(refs, slot, c):
        def act(places, rows):
            for n, ref in enumerate(refs):
                pair = [ref[place, :, lanes_of(c)].astype(jnp.float32) for place in places]
                rows_ref[slot + n, rows, :] = jnp.concatenate(pair, axis=0)

        regroup(act)
        return [rows_ref[slot + n].astype(jnp.bfloat16) for n in range(len(refs))]

    def store(refs, slot, c):
        def act(places, rows):
            for n, ref in enumerate(refs):
                pair = rows_ref[slot + n, rows, :]
                for k, place in enumerate(places):
                    ref[place, :, lanes_of(c)] = pair[4 * k : 4 * k + 4].astype(jnp.bfloat16)

        regroup(act)

    def prepare(c):
        key, value = load((k_ref, v_ref), 0, c)
        f_send[c] = dot(packed_ref[...], jnp.concatenate([key, value], axis=0)).astype(jnp.bfloat16)
        box[c, 0:CELLS, 0:HALF] = key
        box[c, 0:CELLS, HALF:LANES] = value

    def step_first(c):
        on_sides((0, 1), lambda s: frame_copies(0, s, c, lambda copy: copy.start()))

    def step_frames(c):
        pl.when(c == 0)(lambda: arrive(load_frames))
        on_sides((0, 1), lambda s: frames_come(0, s, c))
        got = f_in[c].astype(jnp.float32)
        pad = jnp.zeros((FN - FP - RIM, HALF), jnp.float32)
        for half in (0, 1):
            low = RIM * half
            rims = [got[low : low + RIM], pad, got[PIECE + low : PIECE + low + RIM], pad]
            box[c, FP:HP, HALF * half : HALF * half + HALF] = jnp.concatenate(rims, axis=0).astype(jnp.bfloat16)
        h_send[c] = dot(second_ref[...], box[c, 0:HP, :]).astype(jnp.bfloat16)
        on_sides((2, 3), lambda s: height_copy(s, c).start())

    def step_rows(c):
        on_sides((2, 3), lambda s: come(s, c))
        for s in (4, 5):
            for start, count, there in (TO_PREV, TO_NEXT)[s - 4]:
                at = there - (WN, WP)[s - 4] + 176 * (s - 4)
                w_send[c, at : at + count, :] = box[c, start : start + count, :]
        on_sides((4, 5), lambda s: width_copy(s, c).start())

    def step_attend(c):
        pl.when(c == 0)(lambda: arrive(load_attend))
        on_sides((4, 5), lambda s: come(s, c))
        edges = sum(jnp.where(present, 0, 1 << number) for number, _, _, present in sides)
        open_side = (side_ref[0:1, :] & edges) == 0
        queries, grads = load((q_ref, d_ref), 2, c)
        for g in range(GROUP):
            head = c * GROUP + g
            key_lanes = slice(g * HD, g * HD + HD)
            value_lanes = slice(HALF + g * HD, HALF + g * HD + HD)
            kind = (15 * ext[0, head] - 14) * (3 * ext[1, head] - 2) * ext[2, head]
            kinds = jnp.where(open_side, kind, 0)
            query, grad = queries[:, key_lanes], grads[:, key_lanes]
            key, value = box[c, :, key_lanes], box[c, :, value_lanes]
            scores = dot(query, key, ((1,), (1,)))
            scores = jnp.where((code_ref[...] & kinds) != 0, scores, -1e30)
            top = jnp.max(scores, axis=1, keepdims=True)
            raised = jnp.exp2((scores - top) * (SCALE * LOG2E))
            probs = raised * (1.0 / jnp.sum(raised, axis=1, keepdims=True))
            weights = probs.astype(jnp.bfloat16)
            attended = dot(weights, value).astype(jnp.bfloat16)
            rows_ref[4, :, key_lanes] = attended.astype(jnp.float32)
            delta = jnp.sum(grad.astype(jnp.float32) * attended.astype(jnp.float32), axis=1, keepdims=True)
            dprobs = dot(grad, value, ((1,), (1,)))
            dscores = (probs * (dprobs - delta) * SCALE).astype(jnp.bfloat16)
            rows_ref[5, :, key_lanes] = dot(dscores, key)
            key_part = dot(dscores, query, ((0,), (0,)))
            value_part = dot(weights, grad, ((0,), (0,)))
            for part, lanes in ((key_part, key_lanes), (value_part, value_lanes)):
                acc[c, :, lanes] = part[0:WP]
                w_back[c, :, lanes] = part[WP:PAD].astype(jnp.bfloat16)
        on_sides((4, 5), lambda s: back_copy(s, c).start())
        store((att_out, dq_out), 4, c)
        pl.when(c == CHUNKS - 1)(lambda: [leave(number, 0).start() for number in (0, 1)] and None)

    def step_back_columns(c):
        def take(s):
            come_back(s, c)
            for start, count, there in (TO_PREV, TO_NEXT)[s - 4]:
                low = there - (WN, WP)[s - 4] + 176 * (s - 4)
                acc[c, start : start + count, :] += w_got[c, low : low + count, :].astype(jnp.float32)

        on_sides((4, 5), take)
        h_back[c] = acc[c, HP:WP, :].astype(jnp.bfloat16)
        on_sides((2, 3), lambda s: back_copy(s, c).start())

    def step_back_rows(c):
        pl.when(c == 0)(lambda: arrive(load_back))
        on_sides((2, 3), lambda s: come_back(s, c))
        acc[c, 0:HP, :] += dot(second_t_ref[...], h_got[c])
        rims = [acc[c, low : low + RIM, HALF * half : HALF * half + HALF] for low in (FP, FN) for half in (0, 1)]
        f_back[c] = jnp.concatenate(rims, axis=0).astype(jnp.bfloat16)
        on_sides((0, 1), lambda s: frame_copies(1, s, c, lambda copy: copy.start()))

    def step_back_frames(c):
        on_sides((0, 1), lambda s: frames_come(1, s, c))
        got = f_got[c].astype(jnp.float32)
        halves = [jnp.concatenate([got[low : low + RIM], got[PIECE + low : PIECE + low + RIM]], axis=0) for low in (0, RIM)]
        terms = jnp.concatenate(halves, axis=1).astype(jnp.bfloat16)
        total = acc[c, 0:CELLS, :] + dot(frames_ref[...], terms)
        rows_ref[6] = total[:, 0:HALF]
        rows_ref[7] = total[:, HALF:LANES]
        store((dk_out, dv_out), 6, c)
        for number in (2, 3):
            leave(number, c).start()

    def tick(t, carry):
        for step, lag in zip(
            (
                step_first,
                functools.partial(step_forward, 0),
                step_frames,
                step_rows,
                step_attend,
                prepare,
                step_back_columns,
                step_back_rows,
                functools.partial(step_forward, 1),
                step_back_frames,
            ),
            LAG,
        ):
            c = t - lag
            pl.when((c >= (1 if lag < 0 else 0)) & (c < CHUNKS))(functools.partial(step, c))
        return carry

    arrive(load_first)
    prepare(0)
    pl.semaphore_wait(barrier, greeted)
    lax.fori_loop(0, CHUNKS + LAG[-1], tick, 0)
    for number in (0, 1):
        leave(number, 0).wait()

    def finish(c, carry):
        for number in (2, 3):
            leave(number, c).wait()
        on_sides(range(6), lambda s: all_sent(s, c))
        if shared:
            for way in (0, 1):
                forward(way, c, lambda copy: copy.wait_send())
        return carry

    lax.fori_loop(0, CHUNKS, finish, 0)


def hand_out(*refs):
    for i in range(4):
        refs[4 + i][...] = refs[i][...]


def on_device(queries, keys, values, out_grad, extents):
    flat = [array.transpose(1, 2, 0, 3).reshape(36, 4, HEADS * HD) for array in (queries, keys, values, out_grad)]
    shape = jax.ShapeDtypeStruct((36, 4, HEADS * HD), jnp.bfloat16)
    vmem, place = pl.BlockSpec(memory_space=pltpu.VMEM), pl.BlockSpec(memory_space=pl.ANY)
    wide, narrow = LANES, HALF
    held = [(BOX, wide), (288, narrow), (288, narrow), (192, wide), (352, wide), (352, wide), (192, wide), (288, narrow)]
    held += [(352, wide), (192, wide), (288, narrow)]
    *tables_in, side = [jnp.asarray(table) for table in tables()]
    operands = [*flat, *tables_in]
    results = pl.pallas_call(
        kernel,
        out_shape=(shape,) * 4,
        in_specs=[pl.BlockSpec(memory_space=pltpu.SMEM), vmem] + [place] * 9,
        out_specs=(place,) * 4,
        scratch_shapes=[pltpu.VMEM(operand.shape, operand.dtype) for operand in operands]
        + [pltpu.VMEM(shape.shape, shape.dtype)] * 4
        + [pltpu.VMEM((CHUNKS, *dims), jnp.bfloat16) for dims in held]
        + [
            pltpu.VMEM((2, CHUNKS, RELAYED, HALF), jnp.bfloat16),
            pltpu.VMEM((CHUNKS, WP, LANES), jnp.float32),
            pltpu.VMEM((8, CELLS, HALF), jnp.float32),
            pltpu.SemaphoreType.DMA((20, CHUNKS)),
            pltpu.SemaphoreType.DMA((14, CHUNKS)),
            pltpu.SemaphoreType.DMA((9,)),
            pltpu.SemaphoreType.DMA((4, CHUNKS)),
        ],
        compiler_params=pltpu.CompilerParams(
            collective_id=0, has_side_effects=True, vmem_limit_bytes=60 * 1024 * 1024
        ),
        cost_estimate=pl.CostEstimate(flops=2_500_000_000, bytes_accessed=8_000_000, transcendentals=1_500_000),
    )(extents.T, side, *operands)
    block = pl.BlockSpec((9, 4, HEADS * HD), lambda i: (i, 0, 0))
    results = pl.pallas_call(
        hand_out,
        grid=(4,),
        out_shape=(shape,) * 4,
        in_specs=[block] * 4,
        out_specs=(block,) * 4,
        compiler_params=pltpu.CompilerParams(vmem_limit_bytes=60 * 1024 * 1024),
        cost_estimate=pl.CostEstimate(flops=0, bytes_accessed=3_600_000, transcendentals=0),
    )(*results)
    return tuple(result.reshape(6, 6, 4, HEADS * HD).transpose(2, 0, 1, 3) for result in results)


def solution(mesh):
    spec = P("frame", "height", "width", None)
    return jax.shard_map(
        on_device,
        mesh=mesh,
        in_specs=(spec, spec, spec, spec, P()),
        out_specs=(spec, spec, spec, spec),
        check_vma=False,
    )
```

```python
import functools

import jax
import jax.numpy as jnp
import numpy as np
from jax import lax
from jax.experimental import pallas as pl
from jax.experimental.pallas import tpu as pltpu
from jax.sharding import PartitionSpec as P

HEADS = 12
HD = 128
EXT = 2
TILE = (4, 6, 6)
CELLS = 144
GROUP = 2
CHUNKS = HEADS // GROUP
HALF = GROUP * HD
LANES = 2 * HALF
SCALE = HD**-0.5
LOG2E = 1.4426950408889634
MESH = pl.DeviceIdType.MESH

FP, FN, HP, HN, WP, WN, PAD, BOX = 144, 224, 304, 400, 496, 672, 848, 896
LAG = (0, 1, 2, 3, 4, -1, 5, 6, 7, 8)
RIM, PIECE, DIRECT, RELAYED = 72, 144, 48, 32
TO_NEXT = ((96, 48, WP), (FP + 48, 32, WP + 48), (FN + 48, 32, WP + 80), (HP + 64, 32, WP + 112), (HN + 64, 32, WP + 144))
TO_PREV = ((0, 48, WN), (FP, 32, WN + 48), (FN, 32, WN + 80), (HP, 32, WN + 112), (HN, 32, WN + 144))


def cell_rows():
    own = [(f, h, w) for w in range(6) for h in range(6) for f in range(4)]
    none = [(99, 99, 99)]
    fp = [(f, h, w) for w in range(6) for h in range(6) for f in (-2, -1)] + none * 8
    fn = [(f, h, w) for w in range(6) for h in range(6) for f in (4, 5)] + none * 8
    hp = [(f, h, w) for w in range(6) for h in (-2, -1) for f in range(-2, 6)]
    hn = [(f, h, w) for w in range(6) for h in (6, 7) for f in range(-2, 6)]
    rows = own + fp + fn + hp + hn
    wp = [(f, h, w - 6) if w in (4, 5) else none[0] for s, n, _ in TO_NEXT for f, h, w in rows[s : s + n]]
    wn = [(f, h, w + 6) if w in (0, 1) else none[0] for s, n, _ in TO_PREV for f, h, w in rows[s : s + n]]
    rows = rows + wp + wn + none * (BOX - PAD)
    return np.array(rows, np.int32)


def tables():
    rows = cell_rows()
    where = {tuple(cell): i for i, cell in enumerate(rows[:HP].tolist()) if cell[0] != 99}
    rims = np.zeros((2 * RIM, CELLS), np.float32)
    for i, (f, h, w) in enumerate(rows[FN : FN + RIM].tolist()):
        rims[i, where[(f - 4, h, w)]] = 1
    for i, (f, h, w) in enumerate(rows[FP : FP + RIM].tolist()):
        rims[RIM + i, where[(f + 4, h, w)]] = 1
    packed = np.zeros((2 * PIECE, 2 * CELLS), np.float32)
    for s in range(2):
        packed[s * PIECE : s * PIECE + RIM, :CELLS] = rims[s * RIM : s * RIM + RIM]
        packed[s * PIECE + RIM : s * PIECE + PIECE, CELLS:] = rims[s * RIM : s * RIM + RIM]
    second = np.zeros((192, HP), np.float32)
    for i, (f, h, w) in enumerate(rows[HN : HN + 96].tolist()):
        second[i, where[(f, h - 6, w)]] = 1
    for i, (f, h, w) in enumerate(rows[HP : HP + 96].tolist()):
        second[96 + i, where[(f, h + 6, w)]] = 1
    code = np.full((CELLS, BOX), 255, np.int32)
    for axis, (one, two) in enumerate(((0x0F, 0xF0), (0x33, 0xCC), (0x55, 0xAA))):
        gap = np.abs(rows[:CELLS, None, axis] - rows[None, :, axis])
        code &= np.where(gap <= 1, one, 0) | np.where(gap <= 2, two, 0)
    side = np.zeros((8, BOX), np.int32)
    for axis, size in enumerate(TILE):
        side |= np.where(rows[:, axis] < 0, 1 << (2 * axis), 0)[None].astype(np.int32)
        side |= np.where(rows[:, axis] >= size, 2 << (2 * axis), 0)[None].astype(np.int32)
    as_bf16 = [array.astype(jnp.bfloat16) for array in (packed, second, second.T, rims.T)]
    return (*as_bf16, code, side)


def dot(left, right, sides=((1,), (0,))):
    return lax.dot_general(left, right, (sides, ((), ())), preferred_element_type=jnp.float32)


def kernel(ext, side_ref, *refs):
    (q_hbm, k_hbm, v_hbm, d_hbm, packed_hbm, second_hbm, second_t_hbm, frames_hbm, code_hbm) = refs[:9]
    outs = refs[9:13]
    (q_ref, k_ref, v_ref, d_ref, packed_ref, second_ref, second_t_ref, frames_ref, code_ref) = refs[13:22]
    att_out, dq_out, dk_out, dv_out = results = refs[22:26]
    (box, f_send, f_in, h_send, w_send, w_back, h_back, f_back, w_got, h_got, f_got, by_way, acc, rows_ref) = refs[26:40]
    send_sem, recv_sem, in_sem, out_sem = refs[40:]

    load_first = ((k_hbm, k_ref), (v_hbm, v_ref), (packed_hbm, packed_ref))
    load_frames = ((second_hbm, second_ref),)
    load_attend = ((q_hbm, q_ref), (d_hbm, d_ref), (code_hbm, code_ref))
    load_back = ((second_t_hbm, second_t_ref), (frames_hbm, frames_ref))
    loads = (*load_first, *load_frames, *load_attend, *load_back)

    def operand(pair):
        number = [other[1] is pair[1] for other in loads].index(True)
        return pltpu.make_async_copy(*pair, in_sem.at[number])

    for pair in loads:
        operand(pair).start()

    def arrive(pairs):
        for pair in pairs:
            operand(pair).wait()

    def leave(number, c):
        if number < 2:
            return pltpu.make_async_copy(results[number], outs[number], out_sem.at[number, 0])
        lanes = pl.ds(pl.multiple_of(c * HALF, HALF), HALF)
        return pltpu.make_async_copy(results[number].at[:, :, lanes], outs[number].at[:, :, lanes], out_sem.at[number, c])

    axes = ("frame", "height", "width")
    index = [lax.axis_index(axis) for axis in axes]
    has_prev = [i > 0 for i in index]
    has_next = [i < lax.axis_size(axis) - 1 for i, axis in zip(index, axes)]
    sides = []
    for axis in range(3):
        sides.append((2 * axis, axes[axis], index[axis] - 1, has_prev[axis]))
        sides.append((2 * axis + 1, axes[axis], index[axis] + 1, has_next[axis]))

    frame, frames = index[0], lax.axis_size("frame")
    shared = frames == 8
    low_mid, high_mid = frames // 2 - 1, frames // 2
    crossing = [(frame == high_mid), (frame == low_mid)] if shared else [False, False]
    helpers = (range(low_mid), range(high_mid + 1, frames))

    def copy(src, dst, number, number_there, axis, other, c):
        return pltpu.make_async_remote_copy(
            src_ref=src,
            dst_ref=dst,
            send_sem=send_sem.at[number, c],
            recv_sem=recv_sem.at[number_there, c],
            device_id={axis: other},
            device_id_type=MESH,
        )

    def remote(src, dst, number, s, c):
        _, axis, other, _ = sides[s]
        return copy(src, dst, number, number, axis, other, c)

    box[:, PAD:BOX, :] = jnp.zeros((CHUNKS, BOX - PAD, LANES), jnp.bfloat16)
    backs = ((h_back, h_got, 96), (w_back, w_got, 176))
    regions = ((FP, FN), (FN, HP), (HP, HN), (HN, WP), (WP, WN), (WN, PAD))
    for (number, _, _, present), (low, high) in zip(sides, regions):

        @pl.when(jnp.logical_not(present))
        def _(number=number, low=low, high=high):
            if number < 2:
                at = PIECE * number
                for got in (f_in, f_got):
                    got[:, at : at + PIECE, :] = jnp.zeros((CHUNKS, PIECE, HALF), jnp.bfloat16)
            else:
                box[:, low:high, :] = jnp.zeros((CHUNKS, high - low, LANES), jnp.bfloat16)
            if number in (2, 3):
                at = 96 * (number - 2)
                h_got[:, at : at + 96, :] = jnp.zeros((CHUNKS, 96, LANES), jnp.bfloat16)

    barrier = pltpu.get_barrier_semaphore()
    for _, axis, other, present in sides:

        @pl.when(present)
        def _(axis=axis, other=other):
            pl.semaphore_signal(barrier, inc=1, device_id={axis: other}, device_id_type=MESH)

    greeted = sum(jnp.where(present, 1, 0) for _, _, _, present in sides)
    if shared:
        middle, rest = (low_mid, high_mid), [*helpers[0], *helpers[1]]
        for here in range(frames):
            others = [other for other in (rest if here in middle else middle) if abs(other - here) > 1]

            @pl.when(frame == here)
            def _(others=others):
                for other in others:
                    pl.semaphore_signal(barrier, inc=1, device_id={"frame": other}, device_id_type=MESH)

            greeted = greeted + jnp.where(frame == here, len(others), 0)
    def frame_copies(way, s, c, act):
        src, dst = ((f_send, f_in), (f_back, f_got))[way]
        here, there, number = PIECE * s, PIECE * (1 - s), 6 * way + (s ^ 1)
        if not shared:
            act(remote(src.at[c, pl.ds(here, PIECE)], dst.at[c, pl.ds(there, PIECE)], number, s, c))
            return

        @pl.when(jnp.logical_not(crossing[s]))
        def _():
            act(remote(src.at[c, pl.ds(here, PIECE)], dst.at[c, pl.ds(there, PIECE)], number, s, c))

        @pl.when(crossing[s])
        def _():
            for i, helper in enumerate(helpers[1 - s]):
                part = src.at[c, pl.ds(here + DIRECT + RELAYED * i, RELAYED)]
                act(copy(part, by_way.at[way, c], 12 + 4 * way + i, 12 + way, "frame", helper, c))
            act(remote(src.at[c, pl.ds(here, DIRECT)], dst.at[c, pl.ds(there, DIRECT)], number, s, c))

    def forward(way, c, act):
        low = frame < low_mid
        s = jnp.where(low, 0, 1)
        i = jnp.where(low, frame, frame - (high_mid + 1))
        rows = pl.ds(pl.multiple_of(PIECE * s + DIRECT + RELAYED * i, 16), RELAYED)
        dst = (f_in, f_got)[way].at[c, rows]
        there = jnp.where(low, high_mid, low_mid)
        act(copy(by_way.at[way, c], dst, 15 + 4 * way, 6 * way + s, "frame", there, c))

    def step_forward(way, c):
        if shared:

            @pl.when((frame < low_mid) | (frame > high_mid))
            def _():
                held = by_way.at[way, c]
                come_from = jnp.where(frame < low_mid, low_mid, high_mid)
                copy(held, held, 12 + way, 12 + way, "frame", come_from, c).wait_recv()
                forward(way, c, lambda copy: copy.start())

    def frames_come(way, s, c):
        got = (f_in, f_got)[way].at[c, pl.ds(PIECE * s, PIECE)]
        remote(got, got, 6 * way + s, s, c).wait_recv()

    def height_copy(s, c):
        src = h_send.at[c, pl.ds(96 * (s - 2), 96)]
        return remote(src, box.at[c, pl.ds((HN, HP)[s - 2], 96)], s ^ 1, s, c)

    def width_copy(s, c):
        src = w_send.at[c, pl.ds(176 * (s - 4), 176)]
        return remote(src, box.at[c, pl.ds((WN, WP)[s - 4], 176)], s ^ 1, s, c)

    def back_copy(s, c):
        src, dst, rows = backs[s // 2 - 1]
        low = rows * (s % 2)
        return remote(src.at[c, pl.ds(low, rows)], dst.at[c, pl.ds(rows - low, rows)], 6 + (s ^ 1), s, c)

    def region(s, c):
        return box.at[c, pl.ds(regions[s][0], regions[s][1] - regions[s][0])]

    def come(s, c):
        remote(region(s, c), region(s, c), s, s, c).wait_recv()

    def come_back(s, c):
        _, dst, rows = backs[s // 2 - 1]
        got = dst.at[c, pl.ds(rows * (s % 2), rows)]
        remote(got, got, 6 + s, s, c).wait_recv()

    def all_sent(s, c):
        if s < 2:
            for way in (0, 1):
                frame_copies(way, s, c, lambda copy: copy.wait_send())
        else:
            remote(region(s, c), region(s, c), s ^ 1, s, c).wait_send()
            back_copy(s, c).wait_send()

    def on_sides(group, act):
        for s in group:
            pl.when(sides[s][3])(functools.partial(act, s))

    def regroup(act):
        def column(w, carry):
            for h in (0, 2, 4):
                act((h * 6 + w, h * 6 + 6 + w), pl.ds(pl.multiple_of(w * 24 + 4 * h, 8), 8))
            return carry

        lax.fori_loop(0, 6, column, 0, unroll=True)

    def lanes_of(c):
        return pl.ds(pl.multiple_of(c * HALF, HALF), HALF)

    def load(refs, slot, c):
        def act(places, rows):
            for n, ref in enumerate(refs):
                pair = [ref[place, :, lanes_of(c)].astype(jnp.float32) for place in places]
                rows_ref[slot + n, rows, :] = jnp.concatenate(pair, axis=0)

        regroup(act)
        return [rows_ref[slot + n].astype(jnp.bfloat16) for n in range(len(refs))]

    def store(refs, slot, c):
        def act(places, rows):
            for n, ref in enumerate(refs):
                pair = rows_ref[slot + n, rows, :]
                for k, place in enumerate(places):
                    ref[place, :, lanes_of(c)] = pair[4 * k : 4 * k + 4].astype(jnp.bfloat16)

        regroup(act)

    def prepare(c):
        key, value = load((k_ref, v_ref), 0, c)
        f_send[c] = dot(packed_ref[...], jnp.concatenate([key, value], axis=0)).astype(jnp.bfloat16)
        box[c, 0:CELLS, 0:HALF] = key
        box[c, 0:CELLS, HALF:LANES] = value

    def step_first(c):
        on_sides((0, 1), lambda s: frame_copies(0, s, c, lambda copy: copy.start()))

    def step_frames(c):
        pl.when(c == 0)(lambda: arrive(load_frames))
        on_sides((0, 1), lambda s: frames_come(0, s, c))
        got = f_in[c].astype(jnp.float32)
        pad = jnp.zeros((FN - FP - RIM, HALF), jnp.float32)
        for half in (0, 1):
            low = RIM * half
            rims = [got[low : low + RIM], pad, got[PIECE + low : PIECE + low + RIM], pad]
            box[c, FP:HP, HALF * half : HALF * half + HALF] = jnp.concatenate(rims, axis=0).astype(jnp.bfloat16)
        h_send[c] = dot(second_ref[...], box[c, 0:HP, :]).astype(jnp.bfloat16)
        on_sides((2, 3), lambda s: height_copy(s, c).start())

    def step_rows(c):
        on_sides((2, 3), lambda s: come(s, c))
        for s in (4, 5):
            for start, count, there in (TO_PREV, TO_NEXT)[s - 4]:
                at = there - (WN, WP)[s - 4] + 176 * (s - 4)
                w_send[c, at : at + count, :] = box[c, start : start + count, :]
        on_sides((4, 5), lambda s: width_copy(s, c).start())

    def step_attend(c):
        pl.when(c == 0)(lambda: arrive(load_attend))
        on_sides((4, 5), lambda s: come(s, c))
        edges = sum(jnp.where(present, 0, 1 << number) for number, _, _, present in sides)
        open_side = (side_ref[0:1, :] & edges) == 0
        queries, grads = load((q_ref, d_ref), 2, c)
        for g in range(GROUP):
            head = c * GROUP + g
            key_lanes = slice(g * HD, g * HD + HD)
            value_lanes = slice(HALF + g * HD, HALF + g * HD + HD)
            kind = (15 * ext[0, head] - 14) * (3 * ext[1, head] - 2) * ext[2, head]
            kinds = jnp.where(open_side, kind, 0)
            query, grad = queries[:, key_lanes], grads[:, key_lanes]
            key, value = box[c, :, key_lanes], box[c, :, value_lanes]
            scores = dot(query, key, ((1,), (1,)))
            scores = jnp.where((code_ref[...] & kinds) != 0, scores, -1e30)
            top = jnp.max(scores, axis=1, keepdims=True)
            raised = jnp.exp2((scores - top) * (SCALE * LOG2E))
            probs = raised * (1.0 / jnp.sum(raised, axis=1, keepdims=True))
            weights = probs.astype(jnp.bfloat16)
            attended = dot(weights, value).astype(jnp.bfloat16)
            rows_ref[4, :, key_lanes] = attended.astype(jnp.float32)
            delta = jnp.sum(grad.astype(jnp.float32) * attended.astype(jnp.float32), axis=1, keepdims=True)
            dprobs = dot(grad, value, ((1,), (1,)))
            dscores = (probs * (dprobs - delta) * SCALE).astype(jnp.bfloat16)
            rows_ref[5, :, key_lanes] = dot(dscores, key)
            key_part = dot(dscores, query, ((0,), (0,)))
            value_part = dot(weights, grad, ((0,), (0,)))
            for part, lanes in ((key_part, key_lanes), (value_part, value_lanes)):
                acc[c, :, lanes] = part[0:WP]
                w_back[c, :, lanes] = part[WP:PAD].astype(jnp.bfloat16)
        on_sides((4, 5), lambda s: back_copy(s, c).start())
        store((att_out, dq_out), 4, c)
        pl.when(c == CHUNKS - 1)(lambda: [leave(number, 0).start() for number in (0, 1)] and None)

    def step_back_columns(c):
        def take(s):
            come_back(s, c)
            for start, count, there in (TO_PREV, TO_NEXT)[s - 4]:
                low = there - (WN, WP)[s - 4] + 176 * (s - 4)
                acc[c, start : start + count, :] += w_got[c, low : low + count, :].astype(jnp.float32)

        on_sides((4, 5), take)
        h_back[c] = acc[c, HP:WP, :].astype(jnp.bfloat16)
        on_sides((2, 3), lambda s: back_copy(s, c).start())

    def step_back_rows(c):
        pl.when(c == 0)(lambda: arrive(load_back))
        on_sides((2, 3), lambda s: come_back(s, c))
        acc[c, 0:HP, :] += dot(second_t_ref[...], h_got[c])
        rims = [acc[c, low : low + RIM, HALF * half : HALF * half + HALF] for low in (FP, FN) for half in (0, 1)]
        f_back[c] = jnp.concatenate(rims, axis=0).astype(jnp.bfloat16)
        on_sides((0, 1), lambda s: frame_copies(1, s, c, lambda copy: copy.start()))

    def step_back_frames(c):
        on_sides((0, 1), lambda s: frames_come(1, s, c))
        got = f_got[c].astype(jnp.float32)
        halves = [jnp.concatenate([got[low : low + RIM], got[PIECE + low : PIECE + low + RIM]], axis=0) for low in (0, RIM)]
        terms = jnp.concatenate(halves, axis=1).astype(jnp.bfloat16)
        total = acc[c, 0:CELLS, :] + dot(frames_ref[...], terms)
        rows_ref[6] = total[:, 0:HALF]
        rows_ref[7] = total[:, HALF:LANES]
        store((dk_out, dv_out), 6, c)
        for number in (2, 3):
            leave(number, c).start()

    def tick(t, carry):
        for step, lag in zip(
            (
                step_first,
                functools.partial(step_forward, 0),
                step_frames,
                step_rows,
                step_attend,
                prepare,
                step_back_columns,
                step_back_rows,
                functools.partial(step_forward, 1),
                step_back_frames,
            ),
            LAG,
        ):
            c = t - lag
            pl.when((c >= (1 if lag < 0 else 0)) & (c < CHUNKS))(functools.partial(step, c))
        return carry

    arrive(load_first)
    prepare(0)
    pl.semaphore_wait(barrier, greeted)
    lax.fori_loop(0, CHUNKS + LAG[-1], tick, 0)
    for number in (0, 1):
        leave(number, 0).wait()

    def finish(c, carry):
        for number in (2, 3):
            leave(number, c).wait()
        on_sides(range(6), lambda s: all_sent(s, c))
        if shared:

            @pl.when((frame < low_mid) | (frame > high_mid))
            def _():
                for way in (0, 1):
                    forward(way, c, lambda copy: copy.wait_send())

        return carry

    lax.fori_loop(0, CHUNKS, finish, 0)


def hand_out(*refs):
    come, leave = [], []
    for i in range(4):
        for j in range(2):
            part = pl.ds(18 * j, 18)
            held = refs[8 + i].at[part]
            come.append(pltpu.make_async_copy(refs[i].at[part], held, refs[12].at[i, j]))
            leave.append(pltpu.make_async_copy(held, refs[4 + i].at[part], refs[13].at[i, j]))
    for copy in come:
        copy.start()
    for first, then in zip(come, leave):
        first.wait()
        then.start()
    for copy in leave:
        copy.wait()


def on_device(queries, keys, values, out_grad, extents):
    flat = [array.transpose(1, 2, 0, 3).reshape(36, 4, HEADS * HD) for array in (queries, keys, values, out_grad)]
    shape = jax.ShapeDtypeStruct((36, 4, HEADS * HD), jnp.bfloat16)
    vmem, place = pl.BlockSpec(memory_space=pltpu.VMEM), pl.BlockSpec(memory_space=pl.ANY)
    wide, narrow = LANES, HALF
    held = [(BOX, wide), (288, narrow), (288, narrow), (192, wide), (352, wide), (352, wide), (192, wide), (288, narrow)]
    held += [(352, wide), (192, wide), (288, narrow)]
    *tables_in, side = [jnp.asarray(table) for table in tables()]
    operands = [*flat, *tables_in]
    results = pl.pallas_call(
        kernel,
        out_shape=(shape,) * 4,
        in_specs=[pl.BlockSpec(memory_space=pltpu.SMEM), vmem] + [place] * 9,
        out_specs=(place,) * 4,
        scratch_shapes=[pltpu.VMEM(operand.shape, operand.dtype) for operand in operands]
        + [pltpu.VMEM(shape.shape, shape.dtype)] * 4
        + [pltpu.VMEM((CHUNKS, *dims), jnp.bfloat16) for dims in held]
        + [
            pltpu.VMEM((2, CHUNKS, RELAYED, HALF), jnp.bfloat16),
            pltpu.VMEM((CHUNKS, WP, LANES), jnp.float32),
            pltpu.VMEM((8, CELLS, HALF), jnp.float32),
            pltpu.SemaphoreType.DMA((20, CHUNKS)),
            pltpu.SemaphoreType.DMA((14, CHUNKS)),
            pltpu.SemaphoreType.DMA((9,)),
            pltpu.SemaphoreType.DMA((4, CHUNKS)),
        ],
        compiler_params=pltpu.CompilerParams(
            collective_id=0, has_side_effects=True, vmem_limit_bytes=60 * 1024 * 1024
        ),
        cost_estimate=pl.CostEstimate(flops=2_500_000_000, bytes_accessed=8_000_000, transcendentals=1_500_000),
    )(extents.T, side, *operands)
    results = pl.pallas_call(
        hand_out,
        out_shape=(shape,) * 4,
        in_specs=[place] * 4,
        out_specs=(place,) * 4,
        scratch_shapes=[pltpu.VMEM(shape.shape, shape.dtype)] * 4 + [pltpu.SemaphoreType.DMA((4, 2))] * 2,
        compiler_params=pltpu.CompilerParams(vmem_limit_bytes=60 * 1024 * 1024),
        cost_estimate=pl.CostEstimate(flops=0, bytes_accessed=3_600_000, transcendentals=0),
    )(*results)
    return tuple(result.reshape(6, 6, 4, HEADS * HD).transpose(2, 0, 1, 3) for result in results)


def solution(mesh):
    spec = P("frame", "height", "width", None)
    return jax.shard_map(
        on_device,
        mesh=mesh,
        in_specs=(spec, spec, spec, spec, P()),
        out_specs=(spec, spec, spec, spec),
        check_vma=False,
    )
```

```python
import functools

import jax
import jax.numpy as jnp
import numpy as np
from jax import lax
from jax.experimental import pallas as pl
from jax.experimental.pallas import tpu as pltpu
from jax.sharding import PartitionSpec as P

HEADS = 12
HD = 128
EXT = 2
TILE = (4, 6, 6)
CELLS = 144
PAIRS, PAIR = HEADS // 2, 2 * HD
LANES = 2 * HD
SCALE = HD**-0.5
LOG2E = 1.4426950408889634
MESH = pl.DeviceIdType.MESH

FP, FN, HP, HN, WP, WN, PAD, BOX = 144, 224, 304, 400, 496, 672, 848, 896
LAG = (0, 1, 2, 3, 4, -1, 5, 6, 7, 8)
RIM, PIECE, DIRECT, RELAYED = 72, 144, 48, 32
TO_NEXT = ((96, 48, WP), (FP + 48, 32, WP + 48), (FN + 48, 32, WP + 80), (HP + 64, 32, WP + 112), (HN + 64, 32, WP + 144))
TO_PREV = ((0, 48, WN), (FP, 32, WN + 48), (FN, 32, WN + 80), (HP, 32, WN + 112), (HN, 32, WN + 144))


def cell_rows():
    own = [(f, h, w) for w in range(6) for h in range(6) for f in range(4)]
    none = [(99, 99, 99)]
    fp = [(f, h, w) for w in range(6) for h in range(6) for f in (-2, -1)] + none * 8
    fn = [(f, h, w) for w in range(6) for h in range(6) for f in (4, 5)] + none * 8
    hp = [(f, h, w) for w in range(6) for h in (-2, -1) for f in range(-2, 6)]
    hn = [(f, h, w) for w in range(6) for h in (6, 7) for f in range(-2, 6)]
    rows = own + fp + fn + hp + hn
    wp = [(f, h, w - 6) if w in (4, 5) else none[0] for s, n, _ in TO_NEXT for f, h, w in rows[s : s + n]]
    wn = [(f, h, w + 6) if w in (0, 1) else none[0] for s, n, _ in TO_PREV for f, h, w in rows[s : s + n]]
    rows = rows + wp + wn + none * (BOX - PAD)
    return np.array(rows, np.int32)


def tables():
    rows = cell_rows()
    where = {tuple(cell): i for i, cell in enumerate(rows[:HP].tolist()) if cell[0] != 99}
    rims = np.zeros((2 * RIM, CELLS), np.float32)
    for i, (f, h, w) in enumerate(rows[FN : FN + RIM].tolist()):
        rims[i, where[(f - 4, h, w)]] = 1
    for i, (f, h, w) in enumerate(rows[FP : FP + RIM].tolist()):
        rims[RIM + i, where[(f + 4, h, w)]] = 1
    packed = np.zeros((2 * PIECE, 2 * CELLS), np.float32)
    for s in range(2):
        packed[s * PIECE : s * PIECE + RIM, :CELLS] = rims[s * RIM : s * RIM + RIM]
        packed[s * PIECE + RIM : s * PIECE + PIECE, CELLS:] = rims[s * RIM : s * RIM + RIM]
    second = np.zeros((192, HP), np.float32)
    for i, (f, h, w) in enumerate(rows[HN : HN + 96].tolist()):
        second[i, where[(f, h - 6, w)]] = 1
    for i, (f, h, w) in enumerate(rows[HP : HP + 96].tolist()):
        second[96 + i, where[(f, h + 6, w)]] = 1
    code = np.full((CELLS, BOX), 255, np.int32)
    for axis, (one, two) in enumerate(((0x0F, 0xF0), (0x33, 0xCC), (0x55, 0xAA))):
        gap = np.abs(rows[:CELLS, None, axis] - rows[None, :, axis])
        code &= np.where(gap <= 1, one, 0) | np.where(gap <= 2, two, 0)
    side = np.zeros((8, BOX), np.int32)
    for axis, size in enumerate(TILE):
        side |= np.where(rows[:, axis] < 0, 1 << (2 * axis), 0)[None].astype(np.int32)
        side |= np.where(rows[:, axis] >= size, 2 << (2 * axis), 0)[None].astype(np.int32)
    as_bf16 = [array.astype(jnp.bfloat16) for array in (packed, second, second.T, rims.T)]
    return (*as_bf16, code, side)


def dot(left, right, sides=((1,), (0,))):
    return lax.dot_general(left, right, (sides, ((), ())), preferred_element_type=jnp.float32)


def kernel(ext, side_ref, *refs):
    (q_hbm, k_hbm, v_hbm, d_hbm, packed_hbm, second_hbm, second_t_hbm, frames_hbm, code_hbm) = refs[:9]
    outs = refs[9:13]
    (q_ref, k_ref, v_ref, d_ref, packed_ref, second_ref, second_t_ref, frames_ref, code_ref) = refs[13:22]
    att_out, dq_out, dk_out, dv_out = results = refs[22:26]
    (box, f_send, f_in, h_send, w_send, w_back, h_back, f_back, w_got, h_got, f_got, by_way, acc, rows_ref) = refs[26:40]
    send_sem, recv_sem, in_sem, out_sem = refs[40:]

    load_first = ((k_hbm, k_ref), (v_hbm, v_ref), (packed_hbm, packed_ref))
    load_frames = ((second_hbm, second_ref),)
    load_attend = ((q_hbm, q_ref), (d_hbm, d_ref), (code_hbm, code_ref))
    load_back = ((second_t_hbm, second_t_ref), (frames_hbm, frames_ref))
    loads = (*load_first, *load_frames, *load_attend, *load_back)

    def operand(pair):
        number = [other[1] is pair[1] for other in loads].index(True)
        return pltpu.make_async_copy(*pair, in_sem.at[number])

    for pair in loads:
        operand(pair).start()

    def arrive(pairs):
        for pair in pairs:
            operand(pair).wait()

    def leave(number, j):
        if number < 2:
            return pltpu.make_async_copy(results[number], outs[number], out_sem.at[number, 0])
        lanes = pl.ds(pl.multiple_of(j * PAIR, PAIR), PAIR)
        return pltpu.make_async_copy(results[number].at[:, :, lanes], outs[number].at[:, :, lanes], out_sem.at[number, j])

    axes = ("frame", "height", "width")
    index = [lax.axis_index(axis) for axis in axes]
    has_prev = [i > 0 for i in index]
    has_next = [i < lax.axis_size(axis) - 1 for i, axis in zip(index, axes)]
    sides = []
    for axis in range(3):
        sides.append((2 * axis, axes[axis], index[axis] - 1, has_prev[axis]))
        sides.append((2 * axis + 1, axes[axis], index[axis] + 1, has_next[axis]))

    frame, frames = index[0], lax.axis_size("frame")
    shared = frames == 8
    low_mid, high_mid = frames // 2 - 1, frames // 2
    crossing = [(frame == high_mid), (frame == low_mid)] if shared else [False, False]
    helpers = (range(low_mid), range(high_mid + 1, frames))

    def copy(src, dst, number, number_there, axis, other, c):
        return pltpu.make_async_remote_copy(
            src_ref=src,
            dst_ref=dst,
            send_sem=send_sem.at[number, c],
            recv_sem=recv_sem.at[number_there, c],
            device_id={axis: other},
            device_id_type=MESH,
        )

    def remote(src, dst, number, s, c):
        _, axis, other, _ = sides[s]
        return copy(src, dst, number, number, axis, other, c)

    box[:, PAD:BOX, :] = jnp.zeros((HEADS, BOX - PAD, LANES), jnp.bfloat16)
    backs = ((h_back, h_got, 96), (w_back, w_got, 176))
    regions = ((FP, FN), (FN, HP), (HP, HN), (HN, WP), (WP, WN), (WN, PAD))
    for (number, _, _, present), (low, high) in zip(sides, regions):

        @pl.when(jnp.logical_not(present))
        def _(number=number, low=low, high=high):
            if number < 2:
                at = PIECE * number
                for got in (f_in, f_got):
                    got[:, at : at + PIECE, :] = jnp.zeros((HEADS, PIECE, HD), jnp.bfloat16)
            else:
                box[:, low:high, :] = jnp.zeros((HEADS, high - low, LANES), jnp.bfloat16)
            if number in (2, 3):
                at = 96 * (number - 2)
                h_got[:, at : at + 96, :] = jnp.zeros((HEADS, 96, LANES), jnp.bfloat16)

    barrier = pltpu.get_barrier_semaphore()
    for _, axis, other, present in sides:

        @pl.when(present)
        def _(axis=axis, other=other):
            pl.semaphore_signal(barrier, inc=1, device_id={axis: other}, device_id_type=MESH)

    greeted = sum(jnp.where(present, 1, 0) for _, _, _, present in sides)
    if shared:
        middle, rest = (low_mid, high_mid), [*helpers[0], *helpers[1]]
        for here in range(frames):
            others = [other for other in (rest if here in middle else middle) if abs(other - here) > 1]

            @pl.when(frame == here)
            def _(others=others):
                for other in others:
                    pl.semaphore_signal(barrier, inc=1, device_id={"frame": other}, device_id_type=MESH)

            greeted = greeted + jnp.where(frame == here, len(others), 0)
    def frame_copies(way, s, c, act):
        src, dst = ((f_send, f_in), (f_back, f_got))[way]
        here, there, number = PIECE * s, PIECE * (1 - s), 6 * way + (s ^ 1)
        if not shared:
            act(remote(src.at[c, pl.ds(here, PIECE)], dst.at[c, pl.ds(there, PIECE)], number, s, c))
            return

        @pl.when(jnp.logical_not(crossing[s]))
        def _():
            act(remote(src.at[c, pl.ds(here, PIECE)], dst.at[c, pl.ds(there, PIECE)], number, s, c))

        @pl.when(crossing[s])
        def _():
            for i, helper in enumerate(helpers[1 - s]):
                part = src.at[c, pl.ds(here + DIRECT + RELAYED * i, RELAYED)]
                act(copy(part, by_way.at[way, c], 12 + 4 * way + i, 12 + way, "frame", helper, c))
            act(remote(src.at[c, pl.ds(here, DIRECT)], dst.at[c, pl.ds(there, DIRECT)], number, s, c))

    def forward(way, c, act):
        low = frame < low_mid
        s = jnp.where(low, 0, 1)
        i = jnp.where(low, frame, frame - (high_mid + 1))
        rows = pl.ds(pl.multiple_of(PIECE * s + DIRECT + RELAYED * i, 16), RELAYED)
        dst = (f_in, f_got)[way].at[c, rows]
        there = jnp.where(low, high_mid, low_mid)
        act(copy(by_way.at[way, c], dst, 15 + 4 * way, 6 * way + s, "frame", there, c))

    def step_forward(way, j):
        if shared:

            @pl.when((frame < low_mid) | (frame > high_mid))
            def _():
                come_from = jnp.where(frame < low_mid, low_mid, high_mid)
                for c in (2 * j, 2 * j + 1):
                    held = by_way.at[way, c]
                    copy(held, held, 12 + way, 12 + way, "frame", come_from, c).wait_recv()
                    forward(way, c, lambda copy: copy.start())

    def frames_come(way, s, c):
        got = (f_in, f_got)[way].at[c, pl.ds(PIECE * s, PIECE)]
        remote(got, got, 6 * way + s, s, c).wait_recv()

    def height_copy(s, c):
        src = h_send.at[c, pl.ds(96 * (s - 2), 96)]
        return remote(src, box.at[c, pl.ds((HN, HP)[s - 2], 96)], s ^ 1, s, c)

    def width_copy(s, c):
        src = w_send.at[c, pl.ds(176 * (s - 4), 176)]
        return remote(src, box.at[c, pl.ds((WN, WP)[s - 4], 176)], s ^ 1, s, c)

    def back_copy(s, c):
        src, dst, rows = backs[s // 2 - 1]
        low = rows * (s % 2)
        return remote(src.at[c, pl.ds(low, rows)], dst.at[c, pl.ds(rows - low, rows)], 6 + (s ^ 1), s, c)

    def region(s, c):
        return box.at[c, pl.ds(regions[s][0], regions[s][1] - regions[s][0])]

    def come(s, c):
        remote(region(s, c), region(s, c), s, s, c).wait_recv()

    def come_back(s, c):
        _, dst, rows = backs[s // 2 - 1]
        got = dst.at[c, pl.ds(rows * (s % 2), rows)]
        remote(got, got, 6 + s, s, c).wait_recv()

    def all_sent(s, c):
        if s < 2:
            for way in (0, 1):
                frame_copies(way, s, c, lambda copy: copy.wait_send())
        else:
            remote(region(s, c), region(s, c), s ^ 1, s, c).wait_send()
            back_copy(s, c).wait_send()

    def on_sides(group, act):
        for s in group:
            pl.when(sides[s][3])(functools.partial(act, s))

    def regroup(act):
        def column(w, carry):
            for h in (0, 2, 4):
                act((h * 6 + w, h * 6 + 6 + w), pl.ds(pl.multiple_of(w * 24 + 4 * h, 8), 8))
            return carry

        lax.fori_loop(0, 6, column, 0, unroll=True)

    def lanes_of(j):
        return pl.ds(pl.multiple_of(j * PAIR, PAIR), PAIR)

    def load(refs, slot, j):
        def act(places, rows):
            for n, ref in enumerate(refs):
                pair = [ref[place, :, lanes_of(j)].astype(jnp.float32) for place in places]
                rows_ref[slot + n, rows, :] = jnp.concatenate(pair, axis=0)

        regroup(act)
        return [rows_ref[slot + n].astype(jnp.bfloat16) for n in range(len(refs))]

    def store(refs, slot, j):
        def act(places, rows):
            for n, ref in enumerate(refs):
                pair = rows_ref[slot + n, rows, :]
                for k, place in enumerate(places):
                    ref[place, :, lanes_of(j)] = pair[4 * k : 4 * k + 4].astype(jnp.bfloat16)

        regroup(act)

    def prepare(j):
        keys, values = load((k_ref, v_ref), 0, j)
        for g in (0, 1):
            key, value = keys[:, g * HD : g * HD + HD], values[:, g * HD : g * HD + HD]
            f_send[2 * j + g] = dot(packed_ref[...], jnp.concatenate([key, value], axis=0)).astype(jnp.bfloat16)
            box[2 * j + g, 0:CELLS, 0:HD] = key
            box[2 * j + g, 0:CELLS, HD:LANES] = value

    def each(step):
        def both(j):
            step(2 * j)
            step(2 * j + 1)

        return both

    def step_first(c):
        on_sides((0, 1), lambda s: frame_copies(0, s, c, lambda copy: copy.start()))

    def step_frames(c):
        pl.when(c == 0)(lambda: arrive(load_frames))
        on_sides((0, 1), lambda s: frames_come(0, s, c))
        got = f_in[c].astype(jnp.float32)
        pad = jnp.zeros((FN - FP - RIM, HD), jnp.float32)
        for half in (0, 1):
            low = RIM * half
            rims = [got[low : low + RIM], pad, got[PIECE + low : PIECE + low + RIM], pad]
            box[c, FP:HP, HD * half : HD * half + HD] = jnp.concatenate(rims, axis=0).astype(jnp.bfloat16)
        h_send[c] = dot(second_ref[...], box[c, 0:HP, :]).astype(jnp.bfloat16)
        on_sides((2, 3), lambda s: height_copy(s, c).start())

    def step_rows(c):
        on_sides((2, 3), lambda s: come(s, c))
        for s in (4, 5):
            for start, count, there in (TO_PREV, TO_NEXT)[s - 4]:
                at = there - (WN, WP)[s - 4] + 176 * (s - 4)
                w_send[c, at : at + count, :] = box[c, start : start + count, :]
        on_sides((4, 5), lambda s: width_copy(s, c).start())

    def step_attend(j):
        pl.when(j == 0)(lambda: arrive(load_attend))
        for c in (2 * j, 2 * j + 1):
            on_sides((4, 5), lambda s: come(s, c))
        edges = sum(jnp.where(present, 0, 1 << number) for number, _, _, present in sides)
        open_side = (side_ref[0:1, :] & edges) == 0
        queries, grads = load((q_ref, d_ref), 2, j)
        for g in (0, 1):
            c = 2 * j + g
            lanes = slice(g * HD, g * HD + HD)
            kind = (15 * ext[0, c] - 14) * (3 * ext[1, c] - 2) * ext[2, c]
            kinds = jnp.where(open_side, kind, 0)
            query, grad = queries[:, lanes], grads[:, lanes]
            key, value = box[c, :, 0:HD], box[c, :, HD:LANES]
            scores = dot(query, key, ((1,), (1,)))
            scores = jnp.where((code_ref[...] & kinds) != 0, scores, -1e30)
            top = jnp.max(scores, axis=1, keepdims=True)
            raised = jnp.exp2((scores - top) * (SCALE * LOG2E))
            probs = raised * (1.0 / jnp.sum(raised, axis=1, keepdims=True))
            weights = probs.astype(jnp.bfloat16)
            attended = dot(weights, value).astype(jnp.bfloat16)
            rows_ref[4, :, lanes] = attended.astype(jnp.float32)
            delta = jnp.sum(grad.astype(jnp.float32) * attended.astype(jnp.float32), axis=1, keepdims=True)
            dprobs = dot(grad, value, ((1,), (1,)))
            dscores = (probs * (dprobs - delta) * SCALE).astype(jnp.bfloat16)
            rows_ref[5, :, lanes] = dot(dscores, key)
            key_part = dot(dscores, query, ((0,), (0,)))
            value_part = dot(weights, grad, ((0,), (0,)))
            for part, place in ((key_part, slice(0, HD)), (value_part, slice(HD, LANES))):
                acc[c, :, place] = part[0:WP]
                w_back[c, :, place] = part[WP:PAD].astype(jnp.bfloat16)
        for c in (2 * j, 2 * j + 1):
            on_sides((4, 5), lambda s: back_copy(s, c).start())
        store((att_out, dq_out), 4, j)
        pl.when(j == PAIRS - 1)(lambda: [leave(number, 0).start() for number in (0, 1)] and None)

    def step_back_columns(c):
        def take(s):
            come_back(s, c)
            for start, count, there in (TO_PREV, TO_NEXT)[s - 4]:
                low = there - (WN, WP)[s - 4] + 176 * (s - 4)
                acc[c, start : start + count, :] += w_got[c, low : low + count, :].astype(jnp.float32)

        on_sides((4, 5), take)
        h_back[c] = acc[c, HP:WP, :].astype(jnp.bfloat16)
        on_sides((2, 3), lambda s: back_copy(s, c).start())

    def step_back_rows(c):
        pl.when(c == 0)(lambda: arrive(load_back))
        on_sides((2, 3), lambda s: come_back(s, c))
        acc[c, 0:HP, :] += dot(second_t_ref[...], h_got[c])
        rims = [acc[c, low : low + RIM, HD * half : HD * half + HD] for low in (FP, FN) for half in (0, 1)]
        f_back[c] = jnp.concatenate(rims, axis=0).astype(jnp.bfloat16)
        on_sides((0, 1), lambda s: frame_copies(1, s, c, lambda copy: copy.start()))

    def step_back_frames(j):
        for g in (0, 1):
            c = 2 * j + g
            on_sides((0, 1), lambda s: frames_come(1, s, c))
            got = f_got[c].astype(jnp.float32)
            halves = [
                jnp.concatenate([got[low : low + RIM], got[PIECE + low : PIECE + low + RIM]], axis=0) for low in (0, RIM)
            ]
            terms = jnp.concatenate(halves, axis=1).astype(jnp.bfloat16)
            total = acc[c, 0:CELLS, :] + dot(frames_ref[...], terms)
            rows_ref[6, :, g * HD : g * HD + HD] = total[:, 0:HD]
            rows_ref[7, :, g * HD : g * HD + HD] = total[:, HD:LANES]
        store((dk_out, dv_out), 6, j)
        for number in (2, 3):
            leave(number, j).start()

    def tick(t, carry):
        for step, lag in zip(
            (
                each(step_first),
                functools.partial(step_forward, 0),
                each(step_frames),
                each(step_rows),
                step_attend,
                prepare,
                each(step_back_columns),
                each(step_back_rows),
                functools.partial(step_forward, 1),
                step_back_frames,
            ),
            LAG,
        ):
            j = t - lag
            pl.when((j >= (1 if lag < 0 else 0)) & (j < PAIRS))(functools.partial(step, j))
        return carry

    arrive(load_first)
    prepare(0)
    pl.semaphore_wait(barrier, greeted)
    lax.fori_loop(0, PAIRS + LAG[-1], tick, 0)
    for number in (0, 1):
        leave(number, 0).wait()

    for number in (2, 3):
        for j in range(PAIRS):
            leave(number, j).wait()

    def finish(c, carry):
        on_sides(range(6), lambda s: all_sent(s, c))
        if shared:

            @pl.when((frame < low_mid) | (frame > high_mid))
            def _():
                for way in (0, 1):
                    forward(way, c, lambda copy: copy.wait_send())

        return carry

    lax.fori_loop(0, HEADS, finish, 0)


def hand_out(*refs):
    come, leave = [], []
    for i in range(4):
        for j in range(2):
            part = pl.ds(18 * j, 18)
            held = refs[8 + i].at[part]
            come.append(pltpu.make_async_copy(refs[i].at[part], held, refs[12].at[i, j]))
            leave.append(pltpu.make_async_copy(held, refs[4 + i].at[part], refs[13].at[i, j]))
    for copy in come:
        copy.start()
    for first, then in zip(come, leave):
        first.wait()
        then.start()
    for copy in leave:
        copy.wait()


def on_device(queries, keys, values, out_grad, extents):
    flat = [array.transpose(1, 2, 0, 3).reshape(36, 4, HEADS * HD) for array in (queries, keys, values, out_grad)]
    shape = jax.ShapeDtypeStruct((36, 4, HEADS * HD), jnp.bfloat16)
    vmem, place = pl.BlockSpec(memory_space=pltpu.VMEM), pl.BlockSpec(memory_space=pl.ANY)
    wide, narrow = LANES, HD
    held = [(BOX, wide), (288, narrow), (288, narrow), (192, wide), (352, wide), (352, wide), (192, wide), (288, narrow)]
    held += [(352, wide), (192, wide), (288, narrow)]
    *tables_in, side = [jnp.asarray(table) for table in tables()]
    operands = [*flat, *tables_in]
    results = pl.pallas_call(
        kernel,
        out_shape=(shape,) * 4,
        in_specs=[pl.BlockSpec(memory_space=pltpu.SMEM), vmem] + [place] * 9,
        out_specs=(place,) * 4,
        scratch_shapes=[pltpu.VMEM(operand.shape, operand.dtype) for operand in operands]
        + [pltpu.VMEM(shape.shape, shape.dtype)] * 4
        + [pltpu.VMEM((HEADS, *dims), jnp.bfloat16) for dims in held]
        + [
            pltpu.VMEM((2, HEADS, RELAYED, HD), jnp.bfloat16),
            pltpu.VMEM((HEADS, WP, LANES), jnp.float32),
            pltpu.VMEM((8, CELLS, PAIR), jnp.float32),
            pltpu.SemaphoreType.DMA((20, HEADS)),
            pltpu.SemaphoreType.DMA((14, HEADS)),
            pltpu.SemaphoreType.DMA((9,)),
            pltpu.SemaphoreType.DMA((4, PAIRS)),
        ],
        compiler_params=pltpu.CompilerParams(
            collective_id=0, has_side_effects=True, vmem_limit_bytes=60 * 1024 * 1024
        ),
        cost_estimate=pl.CostEstimate(flops=2_500_000_000, bytes_accessed=8_000_000, transcendentals=1_500_000),
    )(extents.T, side, *operands)
    results = pl.pallas_call(
        hand_out,
        out_shape=(shape,) * 4,
        in_specs=[place] * 4,
        out_specs=(place,) * 4,
        scratch_shapes=[pltpu.VMEM(shape.shape, shape.dtype)] * 4 + [pltpu.SemaphoreType.DMA((4, 2))] * 2,
        compiler_params=pltpu.CompilerParams(vmem_limit_bytes=60 * 1024 * 1024),
        cost_estimate=pl.CostEstimate(flops=0, bytes_accessed=3_600_000, transcendentals=0),
    )(*results)
    return tuple(result.reshape(6, 6, 4, HEADS * HD).transpose(2, 0, 1, 3) for result in results)


def solution(mesh):
    spec = P("frame", "height", "width", None)
    return jax.shard_map(
        on_device,
        mesh=mesh,
        in_specs=(spec, spec, spec, spec, P()),
        out_specs=(spec, spec, spec, spec),
        check_vma=False,
    )
```

```python
import functools

import jax
import jax.numpy as jnp
import numpy as np
from jax import lax
from jax.experimental import pallas as pl
from jax.experimental.pallas import tpu as pltpu
from jax.sharding import PartitionSpec as P

HEADS = 12
HD = 128
EXT = 2
TILE = (4, 6, 6)
CELLS = 144
GROUP = 2
CHUNKS = HEADS // GROUP
HALF = GROUP * HD
LANES = 2 * HALF
SCALE = HD**-0.5
LOG2E = 1.4426950408889634
MESH = pl.DeviceIdType.MESH

FP, FN, HP, HN, WP, WN, PAD, BOX = 144, 224, 304, 400, 496, 672, 848, 896
LAG = (1, 2, 3, 0, 4, -1, 7, 5, 6, 8)
RIM, PIECE, DIRECT, RELAYED = 72, 144, 48, 32
TO_NEXT = ((96, 48, WP), (FP + 48, 32, WP + 48), (FN + 48, 32, WP + 80), (HP + 64, 32, WP + 112), (HN + 64, 32, WP + 144))
TO_PREV = ((0, 48, WN), (FP, 32, WN + 48), (FN, 32, WN + 80), (HP, 32, WN + 112), (HN, 32, WN + 144))


def cell_rows():
    own = [(f, h, w) for w in range(6) for h in range(6) for f in range(4)]
    none = [(99, 99, 99)]
    fp = [(f, h, w) for w in range(6) for h in range(6) for f in (-2, -1)] + none * 8
    fn = [(f, h, w) for w in range(6) for h in range(6) for f in (4, 5)] + none * 8
    hp = [(f, h, w) for w in range(6) for h in (-2, -1) for f in range(-2, 6)]
    hn = [(f, h, w) for w in range(6) for h in (6, 7) for f in range(-2, 6)]
    rows = own + fp + fn + hp + hn
    wp = [(f, h, w - 6) if w in (4, 5) else none[0] for s, n, _ in TO_NEXT for f, h, w in rows[s : s + n]]
    wn = [(f, h, w + 6) if w in (0, 1) else none[0] for s, n, _ in TO_PREV for f, h, w in rows[s : s + n]]
    rows = rows + wp + wn + none * (BOX - PAD)
    return np.array(rows, np.int32)


def tables():
    rows = cell_rows()
    where = {tuple(cell): i for i, cell in enumerate(rows[:HP].tolist()) if cell[0] != 99}
    rims = np.zeros((2 * RIM, CELLS), np.float32)
    for i, (f, h, w) in enumerate(rows[FN : FN + RIM].tolist()):
        rims[i, where[(f - 4, h, w)]] = 1
    for i, (f, h, w) in enumerate(rows[FP : FP + RIM].tolist()):
        rims[RIM + i, where[(f + 4, h, w)]] = 1
    packed = np.zeros((2 * PIECE, 2 * CELLS), np.float32)
    for s in range(2):
        packed[s * PIECE : s * PIECE + RIM, :CELLS] = rims[s * RIM : s * RIM + RIM]
        packed[s * PIECE + RIM : s * PIECE + PIECE, CELLS:] = rims[s * RIM : s * RIM + RIM]
    second = np.zeros((192, HP), np.float32)
    for i, (f, h, w) in enumerate(rows[HN : HN + 96].tolist()):
        second[i, where[(f, h - 6, w)]] = 1
    for i, (f, h, w) in enumerate(rows[HP : HP + 96].tolist()):
        second[96 + i, where[(f, h + 6, w)]] = 1
    code = np.full((CELLS, BOX), 255, np.int32)
    for axis, (one, two) in enumerate(((0x0F, 0xF0), (0x33, 0xCC), (0x55, 0xAA))):
        gap = np.abs(rows[:CELLS, None, axis] - rows[None, :, axis])
        code &= np.where(gap <= 1, one, 0) | np.where(gap <= 2, two, 0)
    side = np.zeros((8, BOX), np.int32)
    for axis, size in enumerate(TILE):
        side |= np.where(rows[:, axis] < 0, 1 << (2 * axis), 0)[None].astype(np.int32)
        side |= np.where(rows[:, axis] >= size, 2 << (2 * axis), 0)[None].astype(np.int32)
    as_bf16 = [array.astype(jnp.bfloat16) for array in (packed, second, second.T, rims.T)]
    return (*as_bf16, code, side)


def dot(left, right, sides=((1,), (0,))):
    return lax.dot_general(left, right, (sides, ((), ())), preferred_element_type=jnp.float32)


def kernel(ext, side_ref, *refs):
    (q_hbm, k_hbm, v_hbm, d_hbm, packed_hbm, second_hbm, second_t_hbm, frames_hbm, code_hbm) = refs[:9]
    outs = refs[9:13]
    (q_ref, k_ref, v_ref, d_ref, packed_ref, second_ref, second_t_ref, frames_ref, code_ref) = refs[13:22]
    att_out, dq_out, dk_out, dv_out = results = refs[22:26]
    (box, f_send, f_in, h_send, w_send, w_back, h_back, f_back, w_got, h_got, f_got, by_way, acc, rows_ref) = refs[26:40]
    send_sem, recv_sem, in_sem, out_sem = refs[40:]

    load_first = ((k_hbm, k_ref), (v_hbm, v_ref), (packed_hbm, packed_ref))
    load_frames = ((second_hbm, second_ref),)
    load_attend = ((q_hbm, q_ref), (d_hbm, d_ref), (code_hbm, code_ref))
    load_back = ((second_t_hbm, second_t_ref), (frames_hbm, frames_ref))
    loads = (*load_first, *load_frames, *load_attend, *load_back)

    def operand(pair):
        number = [other[1] is pair[1] for other in loads].index(True)
        return pltpu.make_async_copy(*pair, in_sem.at[number])

    for pair in loads:
        operand(pair).start()

    def arrive(pairs):
        for pair in pairs:
            operand(pair).wait()

    def leave(number, c):
        if number < 2:
            return pltpu.make_async_copy(results[number], outs[number], out_sem.at[number, 0])
        lanes = pl.ds(pl.multiple_of(c * HALF, HALF), HALF)
        return pltpu.make_async_copy(results[number].at[:, :, lanes], outs[number].at[:, :, lanes], out_sem.at[number, c])

    axes = ("frame", "height", "width")
    index = [lax.axis_index(axis) for axis in axes]
    has_prev = [i > 0 for i in index]
    has_next = [i < lax.axis_size(axis) - 1 for i, axis in zip(index, axes)]
    sides = []
    for axis in range(3):
        sides.append((2 * axis, axes[axis], index[axis] - 1, has_prev[axis]))
        sides.append((2 * axis + 1, axes[axis], index[axis] + 1, has_next[axis]))

    frame, frames = index[0], lax.axis_size("frame")
    shared = frames == 8
    low_mid, high_mid = frames // 2 - 1, frames // 2
    crossing = [(frame == high_mid), (frame == low_mid)] if shared else [False, False]
    helpers = (range(low_mid), range(high_mid + 1, frames))

    def copy(src, dst, number, number_there, axis, other, c):
        return pltpu.make_async_remote_copy(
            src_ref=src,
            dst_ref=dst,
            send_sem=send_sem.at[number, c],
            recv_sem=recv_sem.at[number_there, c],
            device_id={axis: other},
            device_id_type=MESH,
        )

    def remote(src, dst, number, s, c):
        _, axis, other, _ = sides[s]
        return copy(src, dst, number, number, axis, other, c)

    box[:, PAD:BOX, :] = jnp.zeros((CHUNKS, BOX - PAD, LANES), jnp.bfloat16)
    backs = ((h_back, h_got, 96), (w_back, w_got, 176))
    regions = ((FP, FN), (FN, HP), (HP, HN), (HN, WP), (WP, WN), (WN, PAD))
    for (number, _, _, present), (low, high) in zip(sides, regions):

        @pl.when(jnp.logical_not(present))
        def _(number=number, low=low, high=high):
            if number < 2:
                at = PIECE * number
                for got in (f_in, f_got):
                    got[:, at : at + PIECE, :] = jnp.zeros((CHUNKS, PIECE, HALF), jnp.bfloat16)
            else:
                box[:, low:high, :] = jnp.zeros((CHUNKS, high - low, LANES), jnp.bfloat16)
            if number in (2, 3):
                at = 96 * (number - 2)
                h_got[:, at : at + 96, :] = jnp.zeros((CHUNKS, 96, LANES), jnp.bfloat16)

    barrier = pltpu.get_barrier_semaphore()
    for _, axis, other, present in sides:

        @pl.when(present)
        def _(axis=axis, other=other):
            pl.semaphore_signal(barrier, inc=1, device_id={axis: other}, device_id_type=MESH)

    greeted = sum(jnp.where(present, 1, 0) for _, _, _, present in sides)
    if shared:
        middle, rest = (low_mid, high_mid), [*helpers[0], *helpers[1]]
        for here in range(frames):
            others = [other for other in (rest if here in middle else middle) if abs(other - here) > 1]

            @pl.when(frame == here)
            def _(others=others):
                for other in others:
                    pl.semaphore_signal(barrier, inc=1, device_id={"frame": other}, device_id_type=MESH)

            greeted = greeted + jnp.where(frame == here, len(others), 0)
    def frame_copies(way, s, c, act):
        src, dst = ((f_send, f_in), (f_back, f_got))[way]
        here, there, number = PIECE * s, PIECE * (1 - s), 6 * way + (s ^ 1)
        if not shared:
            act(remote(src.at[c, pl.ds(here, PIECE)], dst.at[c, pl.ds(there, PIECE)], number, s, c))
            return

        @pl.when(jnp.logical_not(crossing[s]))
        def _():
            act(remote(src.at[c, pl.ds(here, PIECE)], dst.at[c, pl.ds(there, PIECE)], number, s, c))

        @pl.when(crossing[s])
        def _():
            for i, helper in enumerate(helpers[1 - s]):
                part = src.at[c, pl.ds(here + DIRECT + RELAYED * i, RELAYED)]
                act(copy(part, by_way.at[way, c], 12 + 4 * way + i, 12 + way, "frame", helper, c))
            act(remote(src.at[c, pl.ds(here, DIRECT)], dst.at[c, pl.ds(there, DIRECT)], number, s, c))

    def forward(way, c, act):
        low = frame < low_mid
        s = jnp.where(low, 0, 1)
        i = jnp.where(low, frame, frame - (high_mid + 1))
        rows = pl.ds(pl.multiple_of(PIECE * s + DIRECT + RELAYED * i, 16), RELAYED)
        dst = (f_in, f_got)[way].at[c, rows]
        there = jnp.where(low, high_mid, low_mid)
        act(copy(by_way.at[way, c], dst, 15 + 4 * way, 6 * way + s, "frame", there, c))

    def step_forward(way, c):
        if shared:

            @pl.when((frame < low_mid) | (frame > high_mid))
            def _():
                held = by_way.at[way, c]
                come_from = jnp.where(frame < low_mid, low_mid, high_mid)
                copy(held, held, 12 + way, 12 + way, "frame", come_from, c).wait_recv()
                forward(way, c, lambda copy: copy.start())

    def frames_come(way, s, c):
        got = (f_in, f_got)[way].at[c, pl.ds(PIECE * s, PIECE)]
        remote(got, got, 6 * way + s, s, c).wait_recv()

    def height_copy(s, c):
        src = h_send.at[c, pl.ds(96 * (s - 2), 96)]
        return remote(src, box.at[c, pl.ds((HN, HP)[s - 2], 96)], s ^ 1, s, c)

    def width_copy(s, c):
        src = w_send.at[c, pl.ds(176 * (s - 4), 176)]
        return remote(src, box.at[c, pl.ds((WN, WP)[s - 4], 176)], s ^ 1, s, c)

    def back_copy(s, c):
        src, dst, rows = backs[s // 2 - 1]
        low = rows * (s % 2)
        return remote(src.at[c, pl.ds(low, rows)], dst.at[c, pl.ds(rows - low, rows)], 6 + (s ^ 1), s, c)

    def region(s, c):
        return box.at[c, pl.ds(regions[s][0], regions[s][1] - regions[s][0])]

    def come(s, c):
        remote(region(s, c), region(s, c), s, s, c).wait_recv()

    def come_back(s, c):
        _, dst, rows = backs[s // 2 - 1]
        got = dst.at[c, pl.ds(rows * (s % 2), rows)]
        remote(got, got, 6 + s, s, c).wait_recv()

    def all_sent(s, c):
        if s < 2:
            for way in (0, 1):
                frame_copies(way, s, c, lambda copy: copy.wait_send())
        else:
            remote(region(s, c), region(s, c), s ^ 1, s, c).wait_send()
            back_copy(s, c).wait_send()

    def on_sides(group, act):
        for s in group:
            pl.when(sides[s][3])(functools.partial(act, s))

    def regroup(act):
        def column(w, carry):
            for h in (0, 2, 4):
                act((h * 6 + w, h * 6 + 6 + w), pl.ds(pl.multiple_of(w * 24 + 4 * h, 8), 8))
            return carry

        lax.fori_loop(0, 6, column, 0, unroll=True)

    def lanes_of(c):
        return pl.ds(pl.multiple_of(c * HALF, HALF), HALF)

    def load(refs, slot, c):
        def act(places, rows):
            for n, ref in enumerate(refs):
                pair = [ref[place, :, lanes_of(c)].astype(jnp.float32) for place in places]
                rows_ref[slot + n, rows, :] = jnp.concatenate(pair, axis=0)

        regroup(act)
        return [rows_ref[slot + n].astype(jnp.bfloat16) for n in range(len(refs))]

    def store(refs, slot, c):
        def act(places, rows):
            for n, ref in enumerate(refs):
                pair = rows_ref[slot + n, rows, :]
                for k, place in enumerate(places):
                    ref[place, :, lanes_of(c)] = pair[4 * k : 4 * k + 4].astype(jnp.bfloat16)

        regroup(act)

    def prepare(c):
        key, value = load((k_ref, v_ref), 0, c)
        f_send[c] = dot(packed_ref[...], jnp.concatenate([key, value], axis=0)).astype(jnp.bfloat16)
        box[c, 0:CELLS, 0:HALF] = key
        box[c, 0:CELLS, HALF:LANES] = value

    def step_first(c):
        on_sides((0, 1), lambda s: frame_copies(0, s, c, lambda copy: copy.start()))

    def step_frames(c):
        pl.when(c == 0)(lambda: arrive(load_frames))
        on_sides((0, 1), lambda s: frames_come(0, s, c))
        got = f_in[c].astype(jnp.float32)
        pad = jnp.zeros((FN - FP - RIM, HALF), jnp.float32)
        for half in (0, 1):
            low = RIM * half
            rims = [got[low : low + RIM], pad, got[PIECE + low : PIECE + low + RIM], pad]
            box[c, FP:HP, HALF * half : HALF * half + HALF] = jnp.concatenate(rims, axis=0).astype(jnp.bfloat16)
        h_send[c] = dot(second_ref[...], box[c, 0:HP, :]).astype(jnp.bfloat16)
        on_sides((2, 3), lambda s: height_copy(s, c).start())

    def step_rows(c):
        on_sides((2, 3), lambda s: come(s, c))
        for s in (4, 5):
            for start, count, there in (TO_PREV, TO_NEXT)[s - 4]:
                at = there - (WN, WP)[s - 4] + 176 * (s - 4)
                w_send[c, at : at + count, :] = box[c, start : start + count, :]
        on_sides((4, 5), lambda s: width_copy(s, c).start())

    def step_attend(c):
        pl.when(c == 0)(lambda: arrive(load_attend))
        on_sides((4, 5), lambda s: come(s, c))
        edges = sum(jnp.where(present, 0, 1 << number) for number, _, _, present in sides)
        open_side = (side_ref[0:1, :] & edges) == 0
        queries, grads = load((q_ref, d_ref), 2, c)
        for g in range(GROUP):
            head = c * GROUP + g
            key_lanes = slice(g * HD, g * HD + HD)
            value_lanes = slice(HALF + g * HD, HALF + g * HD + HD)
            kind = (15 * ext[0, head] - 14) * (3 * ext[1, head] - 2) * ext[2, head]
            kinds = jnp.where(open_side, kind, 0)
            query, grad = queries[:, key_lanes], grads[:, key_lanes]
            key, value = box[c, :, key_lanes], box[c, :, value_lanes]
            scores = dot(query, key, ((1,), (1,)))
            scores = jnp.where((code_ref[...] & kinds) != 0, scores, -1e30)
            top = jnp.max(scores, axis=1, keepdims=True)
            raised = jnp.exp2((scores - top) * (SCALE * LOG2E))
            probs = raised * (1.0 / jnp.sum(raised, axis=1, keepdims=True))
            weights = probs.astype(jnp.bfloat16)
            attended = dot(weights, value).astype(jnp.bfloat16)
            rows_ref[4, :, key_lanes] = attended.astype(jnp.float32)
            delta = jnp.sum(grad.astype(jnp.float32) * attended.astype(jnp.float32), axis=1, keepdims=True)
            dprobs = dot(grad, value, ((1,), (1,)))
            dscores = (probs * (dprobs - delta) * SCALE).astype(jnp.bfloat16)
            rows_ref[5, :, key_lanes] = dot(dscores, key)
            key_part = dot(dscores, query, ((0,), (0,)))
            value_part = dot(weights, grad, ((0,), (0,)))
            for part, lanes in ((key_part, key_lanes), (value_part, value_lanes)):
                acc[c, :, lanes] = part[0:WP]
                w_back[c, :, lanes] = part[WP:PAD].astype(jnp.bfloat16)
        on_sides((4, 5), lambda s: back_copy(s, c).start())
        store((att_out, dq_out), 4, c)
        pl.when(c == CHUNKS - 1)(lambda: [leave(number, 0).start() for number in (0, 1)] and None)

    def step_back_columns(c):
        def take(s):
            come_back(s, c)
            for start, count, there in (TO_PREV, TO_NEXT)[s - 4]:
                low = there - (WN, WP)[s - 4] + 176 * (s - 4)
                acc[c, start : start + count, :] += w_got[c, low : low + count, :].astype(jnp.float32)

        on_sides((4, 5), take)
        h_back[c] = acc[c, HP:WP, :].astype(jnp.bfloat16)
        on_sides((2, 3), lambda s: back_copy(s, c).start())

    def step_back_rows(c):
        pl.when(c == 0)(lambda: arrive(load_back))
        on_sides((2, 3), lambda s: come_back(s, c))
        acc[c, 0:HP, :] += dot(second_t_ref[...], h_got[c])
        rims = [acc[c, low : low + RIM, HALF * half : HALF * half + HALF] for low in (FP, FN) for half in (0, 1)]
        f_back[c] = jnp.concatenate(rims, axis=0).astype(jnp.bfloat16)
        on_sides((0, 1), lambda s: frame_copies(1, s, c, lambda copy: copy.start()))

    def step_back_frames(c):
        on_sides((0, 1), lambda s: frames_come(1, s, c))
        got = f_got[c].astype(jnp.float32)
        halves = [jnp.concatenate([got[low : low + RIM], got[PIECE + low : PIECE + low + RIM]], axis=0) for low in (0, RIM)]
        terms = jnp.concatenate(halves, axis=1).astype(jnp.bfloat16)
        total = acc[c, 0:CELLS, :] + dot(frames_ref[...], terms)
        rows_ref[6] = total[:, 0:HALF]
        rows_ref[7] = total[:, HALF:LANES]
        store((dk_out, dv_out), 6, c)
        for number in (2, 3):
            leave(number, c).start()

    def tick(t, carry):
        for step, lag in zip(
            (
                functools.partial(step_forward, 0),
                step_frames,
                step_rows,
                step_first,
                step_attend,
                prepare,
                functools.partial(step_forward, 1),
                step_back_columns,
                step_back_rows,
                step_back_frames,
            ),
            LAG,
        ):
            c = t - lag
            pl.when((c >= (1 if lag < 0 else 0)) & (c < CHUNKS))(functools.partial(step, c))
        return carry

    arrive(load_first)
    prepare(0)
    pl.semaphore_wait(barrier, greeted)
    lax.fori_loop(0, CHUNKS + LAG[-1], tick, 0)
    for number in (0, 1):
        leave(number, 0).wait()

    def finish(c, carry):
        for number in (2, 3):
            leave(number, c).wait()
        on_sides(range(6), lambda s: all_sent(s, c))
        if shared:

            @pl.when((frame < low_mid) | (frame > high_mid))
            def _():
                for way in (0, 1):
                    forward(way, c, lambda copy: copy.wait_send())

        return carry

    lax.fori_loop(0, CHUNKS, finish, 0)


def hand_out(*refs):
    come, leave = [], []
    for i in range(4):
        for j in range(2):
            part = pl.ds(18 * j, 18)
            held = refs[8 + i].at[part]
            come.append(pltpu.make_async_copy(refs[i].at[part], held, refs[12].at[i, j]))
            leave.append(pltpu.make_async_copy(held, refs[4 + i].at[part], refs[13].at[i, j]))
    for copy in come:
        copy.start()
    for first, then in zip(come, leave):
        first.wait()
        then.start()
    for copy in leave:
        copy.wait()


def on_device(queries, keys, values, out_grad, extents):
    flat = [array.transpose(1, 2, 0, 3).reshape(36, 4, HEADS * HD) for array in (queries, keys, values, out_grad)]
    shape = jax.ShapeDtypeStruct((36, 4, HEADS * HD), jnp.bfloat16)
    vmem, place = pl.BlockSpec(memory_space=pltpu.VMEM), pl.BlockSpec(memory_space=pl.ANY)
    wide, narrow = LANES, HALF
    held = [(BOX, wide), (288, narrow), (288, narrow), (192, wide), (352, wide), (352, wide), (192, wide), (288, narrow)]
    held += [(352, wide), (192, wide), (288, narrow)]
    *tables_in, side = [jnp.asarray(table) for table in tables()]
    operands = [*flat, *tables_in]
    results = pl.pallas_call(
        kernel,
        out_shape=(shape,) * 4,
        in_specs=[pl.BlockSpec(memory_space=pltpu.SMEM), vmem] + [place] * 9,
        out_specs=(place,) * 4,
        scratch_shapes=[pltpu.VMEM(operand.shape, operand.dtype) for operand in operands]
        + [pltpu.VMEM(shape.shape, shape.dtype)] * 4
        + [pltpu.VMEM((CHUNKS, *dims), jnp.bfloat16) for dims in held]
        + [
            pltpu.VMEM((2, CHUNKS, RELAYED, HALF), jnp.bfloat16),
            pltpu.VMEM((CHUNKS, WP, LANES), jnp.float32),
            pltpu.VMEM((8, CELLS, HALF), jnp.float32),
            pltpu.SemaphoreType.DMA((20, CHUNKS)),
            pltpu.SemaphoreType.DMA((14, CHUNKS)),
            pltpu.SemaphoreType.DMA((9,)),
            pltpu.SemaphoreType.DMA((4, CHUNKS)),
        ],
        compiler_params=pltpu.CompilerParams(
            collective_id=0, has_side_effects=True, vmem_limit_bytes=60 * 1024 * 1024
        ),
        cost_estimate=pl.CostEstimate(flops=2_500_000_000, bytes_accessed=8_000_000, transcendentals=1_500_000),
    )(extents.T, side, *operands)
    results = pl.pallas_call(
        hand_out,
        out_shape=(shape,) * 4,
        in_specs=[place] * 4,
        out_specs=(place,) * 4,
        scratch_shapes=[pltpu.VMEM(shape.shape, shape.dtype)] * 4 + [pltpu.SemaphoreType.DMA((4, 2))] * 2,
        compiler_params=pltpu.CompilerParams(vmem_limit_bytes=60 * 1024 * 1024),
        cost_estimate=pl.CostEstimate(flops=0, bytes_accessed=3_600_000, transcendentals=0),
    )(*results)
    return tuple(result.reshape(6, 6, 4, HEADS * HD).transpose(2, 0, 1, 3) for result in results)


def solution(mesh):
    spec = P("frame", "height", "width", None)
    return jax.shard_map(
        on_device,
        mesh=mesh,
        in_specs=(spec, spec, spec, spec, P()),
        out_specs=(spec, spec, spec, spec),
        check_vma=False,
    )
```

```python
import functools

import jax
import jax.numpy as jnp
import numpy as np
from jax import lax
from jax.experimental import pallas as pl
from jax.experimental.pallas import tpu as pltpu
from jax.sharding import PartitionSpec as P

HEADS = 12
HD = 128
EXT = 2
TILE = (4, 6, 6)
CELLS = 144
GROUP = 2
CHUNKS = HEADS // GROUP
HALF = GROUP * HD
LANES = 2 * HALF
SCALE = HD**-0.5
LOG2E = 1.4426950408889634
MESH = pl.DeviceIdType.MESH

FP, FN, HP, HN, WP, WN, PAD, BOX = 144, 224, 304, 400, 496, 672, 848, 896
LAG = (-1, 0, 2, 3, 4, -2, 5, 6, 7, 8)
RIM, PIECE, DIRECT, RELAYED = 72, 144, 48, 32
TO_NEXT = ((96, 48, WP), (FP + 48, 32, WP + 48), (FN + 48, 32, WP + 80), (HP + 64, 32, WP + 112), (HN + 64, 32, WP + 144))
TO_PREV = ((0, 48, WN), (FP, 32, WN + 48), (FN, 32, WN + 80), (HP, 32, WN + 112), (HN, 32, WN + 144))


def cell_rows():
    own = [(f, h, w) for w in range(6) for h in range(6) for f in range(4)]
    none = [(99, 99, 99)]
    fp = [(f, h, w) for w in range(6) for h in range(6) for f in (-2, -1)] + none * 8
    fn = [(f, h, w) for w in range(6) for h in range(6) for f in (4, 5)] + none * 8
    hp = [(f, h, w) for w in range(6) for h in (-2, -1) for f in range(-2, 6)]
    hn = [(f, h, w) for w in range(6) for h in (6, 7) for f in range(-2, 6)]
    rows = own + fp + fn + hp + hn
    wp = [(f, h, w - 6) if w in (4, 5) else none[0] for s, n, _ in TO_NEXT for f, h, w in rows[s : s + n]]
    wn = [(f, h, w + 6) if w in (0, 1) else none[0] for s, n, _ in TO_PREV for f, h, w in rows[s : s + n]]
    rows = rows + wp + wn + none * (BOX - PAD)
    return np.array(rows, np.int32)


def tables():
    rows = cell_rows()
    where = {tuple(cell): i for i, cell in enumerate(rows[:HP].tolist()) if cell[0] != 99}
    rims = np.zeros((2 * RIM, CELLS), np.float32)
    for i, (f, h, w) in enumerate(rows[FN : FN + RIM].tolist()):
        rims[i, where[(f - 4, h, w)]] = 1
    for i, (f, h, w) in enumerate(rows[FP : FP + RIM].tolist()):
        rims[RIM + i, where[(f + 4, h, w)]] = 1
    packed = np.zeros((2 * PIECE, 2 * CELLS), np.float32)
    for s in range(2):
        packed[s * PIECE : s * PIECE + RIM, :CELLS] = rims[s * RIM : s * RIM + RIM]
        packed[s * PIECE + RIM : s * PIECE + PIECE, CELLS:] = rims[s * RIM : s * RIM + RIM]
    second = np.zeros((192, HP), np.float32)
    for i, (f, h, w) in enumerate(rows[HN : HN + 96].tolist()):
        second[i, where[(f, h - 6, w)]] = 1
    for i, (f, h, w) in enumerate(rows[HP : HP + 96].tolist()):
        second[96 + i, where[(f, h + 6, w)]] = 1
    code = np.full((CELLS, BOX), 255, np.int32)
    for axis, (one, two) in enumerate(((0x0F, 0xF0), (0x33, 0xCC), (0x55, 0xAA))):
        gap = np.abs(rows[:CELLS, None, axis] - rows[None, :, axis])
        code &= np.where(gap <= 1, one, 0) | np.where(gap <= 2, two, 0)
    side = np.zeros((8, BOX), np.int32)
    for axis, size in enumerate(TILE):
        side |= np.where(rows[:, axis] < 0, 1 << (2 * axis), 0)[None].astype(np.int32)
        side |= np.where(rows[:, axis] >= size, 2 << (2 * axis), 0)[None].astype(np.int32)
    as_bf16 = [array.astype(jnp.bfloat16) for array in (packed, second, second.T, rims.T)]
    return (*as_bf16, code, side)


def dot(left, right, sides=((1,), (0,))):
    return lax.dot_general(left, right, (sides, ((), ())), preferred_element_type=jnp.float32)


def kernel(ext, side_ref, *refs):
    (q_hbm, k_hbm, v_hbm, d_hbm, packed_hbm, second_hbm, second_t_hbm, frames_hbm, code_hbm) = refs[:9]
    outs = refs[9:13]
    (q_ref, k_ref, v_ref, d_ref, packed_ref, second_ref, second_t_ref, frames_ref, code_ref) = refs[13:22]
    att_out, dq_out, dk_out, dv_out = results = refs[22:26]
    (box, f_send, f_in, h_send, w_send, w_back, h_back, f_back, w_got, h_got, f_got, by_way, acc, rows_ref) = refs[26:40]
    send_sem, recv_sem, in_sem, out_sem = refs[40:]

    load_first = ((k_hbm, k_ref), (v_hbm, v_ref), (packed_hbm, packed_ref))
    load_frames = ((second_hbm, second_ref),)
    load_attend = ((q_hbm, q_ref), (d_hbm, d_ref), (code_hbm, code_ref))
    load_back = ((second_t_hbm, second_t_ref), (frames_hbm, frames_ref))
    loads = (*load_first, *load_frames, *load_attend, *load_back)

    def operand(pair):
        number = [other[1] is pair[1] for other in loads].index(True)
        return pltpu.make_async_copy(*pair, in_sem.at[number])

    for pair in loads:
        operand(pair).start()

    def arrive(pairs):
        for pair in pairs:
            operand(pair).wait()

    def leave(number, c):
        if number < 2:
            return pltpu.make_async_copy(results[number], outs[number], out_sem.at[number, 0])
        lanes = pl.ds(pl.multiple_of(c * HALF, HALF), HALF)
        return pltpu.make_async_copy(results[number].at[:, :, lanes], outs[number].at[:, :, lanes], out_sem.at[number, c])

    axes = ("frame", "height", "width")
    index = [lax.axis_index(axis) for axis in axes]
    has_prev = [i > 0 for i in index]
    has_next = [i < lax.axis_size(axis) - 1 for i, axis in zip(index, axes)]
    sides = []
    for axis in range(3):
        sides.append((2 * axis, axes[axis], index[axis] - 1, has_prev[axis]))
        sides.append((2 * axis + 1, axes[axis], index[axis] + 1, has_next[axis]))

    frame, frames = index[0], lax.axis_size("frame")
    shared = frames == 8
    low_mid, high_mid = frames // 2 - 1, frames // 2
    crossing = [(frame == high_mid), (frame == low_mid)] if shared else [False, False]
    helpers = (range(low_mid), range(high_mid + 1, frames))

    def copy(src, dst, number, number_there, axis, other, c):
        return pltpu.make_async_remote_copy(
            src_ref=src,
            dst_ref=dst,
            send_sem=send_sem.at[number, c],
            recv_sem=recv_sem.at[number_there, c],
            device_id={axis: other},
            device_id_type=MESH,
        )

    def remote(src, dst, number, s, c):
        _, axis, other, _ = sides[s]
        return copy(src, dst, number, number, axis, other, c)

    box[:, PAD:BOX, :] = jnp.zeros((CHUNKS, BOX - PAD, LANES), jnp.bfloat16)
    backs = ((h_back, h_got, 96), (w_back, w_got, 176))
    regions = ((FP, FN), (FN, HP), (HP, HN), (HN, WP), (WP, WN), (WN, PAD))
    for (number, _, _, present), (low, high) in zip(sides, regions):

        @pl.when(jnp.logical_not(present))
        def _(number=number, low=low, high=high):
            if number < 2:
                at = PIECE * number
                for got in (f_in, f_got):
                    got[:, at : at + PIECE, :] = jnp.zeros((CHUNKS, PIECE, HALF), jnp.bfloat16)
            else:
                box[:, low:high, :] = jnp.zeros((CHUNKS, high - low, LANES), jnp.bfloat16)
            if number in (2, 3):
                at = 96 * (number - 2)
                h_got[:, at : at + 96, :] = jnp.zeros((CHUNKS, 96, LANES), jnp.bfloat16)

    barrier = pltpu.get_barrier_semaphore()
    for _, axis, other, present in sides:

        @pl.when(present)
        def _(axis=axis, other=other):
            pl.semaphore_signal(barrier, inc=1, device_id={axis: other}, device_id_type=MESH)

    greeted = sum(jnp.where(present, 1, 0) for _, _, _, present in sides)
    if shared:
        middle, rest = (low_mid, high_mid), [*helpers[0], *helpers[1]]
        for here in range(frames):
            others = [other for other in (rest if here in middle else middle) if abs(other - here) > 1]

            @pl.when(frame == here)
            def _(others=others):
                for other in others:
                    pl.semaphore_signal(barrier, inc=1, device_id={"frame": other}, device_id_type=MESH)

            greeted = greeted + jnp.where(frame == here, len(others), 0)
    def frame_copies(way, s, c, act):
        src, dst = ((f_send, f_in), (f_back, f_got))[way]
        here, there, number = PIECE * s, PIECE * (1 - s), 6 * way + (s ^ 1)
        if not shared:
            act(remote(src.at[c, pl.ds(here, PIECE)], dst.at[c, pl.ds(there, PIECE)], number, s, c))
            return

        @pl.when(jnp.logical_not(crossing[s]))
        def _():
            act(remote(src.at[c, pl.ds(here, PIECE)], dst.at[c, pl.ds(there, PIECE)], number, s, c))

        @pl.when(crossing[s])
        def _():
            for i, helper in enumerate(helpers[1 - s]):
                part = src.at[c, pl.ds(here + DIRECT + RELAYED * i, RELAYED)]
                act(copy(part, by_way.at[way, c], 12 + 4 * way + i, 12 + way, "frame", helper, c))
            act(remote(src.at[c, pl.ds(here, DIRECT)], dst.at[c, pl.ds(there, DIRECT)], number, s, c))

    def forward(way, c, act):
        low = frame < low_mid
        s = jnp.where(low, 0, 1)
        i = jnp.where(low, frame, frame - (high_mid + 1))
        rows = pl.ds(pl.multiple_of(PIECE * s + DIRECT + RELAYED * i, 16), RELAYED)
        dst = (f_in, f_got)[way].at[c, rows]
        there = jnp.where(low, high_mid, low_mid)
        act(copy(by_way.at[way, c], dst, 15 + 4 * way, 6 * way + s, "frame", there, c))

    def step_forward(way, c):
        if shared:

            @pl.when((frame < low_mid) | (frame > high_mid))
            def _():
                held = by_way.at[way, c]
                come_from = jnp.where(frame < low_mid, low_mid, high_mid)
                copy(held, held, 12 + way, 12 + way, "frame", come_from, c).wait_recv()
                forward(way, c, lambda copy: copy.start())

    def frames_come(way, s, c):
        got = (f_in, f_got)[way].at[c, pl.ds(PIECE * s, PIECE)]
        remote(got, got, 6 * way + s, s, c).wait_recv()

    def height_copy(s, c):
        src = h_send.at[c, pl.ds(96 * (s - 2), 96)]
        return remote(src, box.at[c, pl.ds((HN, HP)[s - 2], 96)], s ^ 1, s, c)

    def width_copy(s, c):
        src = w_send.at[c, pl.ds(176 * (s - 4), 176)]
        return remote(src, box.at[c, pl.ds((WN, WP)[s - 4], 176)], s ^ 1, s, c)

    def back_copy(s, c):
        src, dst, rows = backs[s // 2 - 1]
        low = rows * (s % 2)
        return remote(src.at[c, pl.ds(low, rows)], dst.at[c, pl.ds(rows - low, rows)], 6 + (s ^ 1), s, c)

    def region(s, c):
        return box.at[c, pl.ds(regions[s][0], regions[s][1] - regions[s][0])]

    def come(s, c):
        remote(region(s, c), region(s, c), s, s, c).wait_recv()

    def come_back(s, c):
        _, dst, rows = backs[s // 2 - 1]
        got = dst.at[c, pl.ds(rows * (s % 2), rows)]
        remote(got, got, 6 + s, s, c).wait_recv()

    def all_sent(s, c):
        if s < 2:
            for way in (0, 1):
                frame_copies(way, s, c, lambda copy: copy.wait_send())
        else:
            remote(region(s, c), region(s, c), s ^ 1, s, c).wait_send()
            back_copy(s, c).wait_send()

    def on_sides(group, act):
        for s in group:
            pl.when(sides[s][3])(functools.partial(act, s))

    def regroup(act):
        def column(w, carry):
            for h in (0, 2, 4):
                act((h * 6 + w, h * 6 + 6 + w), pl.ds(pl.multiple_of(w * 24 + 4 * h, 8), 8))
            return carry

        lax.fori_loop(0, 6, column, 0, unroll=True)

    def lanes_of(c):
        return pl.ds(pl.multiple_of(c * HALF, HALF), HALF)

    def load(refs, slot, c):
        def act(places, rows):
            for n, ref in enumerate(refs):
                pair = [ref[place, :, lanes_of(c)].astype(jnp.float32) for place in places]
                rows_ref[slot + n, rows, :] = jnp.concatenate(pair, axis=0)

        regroup(act)
        return [rows_ref[slot + n].astype(jnp.bfloat16) for n in range(len(refs))]

    def store(refs, slot, c):
        def act(places, rows):
            for n, ref in enumerate(refs):
                pair = rows_ref[slot + n, rows, :]
                for k, place in enumerate(places):
                    ref[place, :, lanes_of(c)] = pair[4 * k : 4 * k + 4].astype(jnp.bfloat16)

        regroup(act)

    def prepare(c):
        key, value = load((k_ref, v_ref), 0, c)
        f_send[c] = dot(packed_ref[...], jnp.concatenate([key, value], axis=0)).astype(jnp.bfloat16)
        box[c, 0:CELLS, 0:HALF] = key
        box[c, 0:CELLS, HALF:LANES] = value

    def step_first(c):
        on_sides((0, 1), lambda s: frame_copies(0, s, c, lambda copy: copy.start()))

    def step_frames(c):
        pl.when(c == 0)(lambda: arrive(load_frames))
        on_sides((0, 1), lambda s: frames_come(0, s, c))
        got = f_in[c].astype(jnp.float32)
        pad = jnp.zeros((FN - FP - RIM, HALF), jnp.float32)
        for half in (0, 1):
            low = RIM * half
            rims = [got[low : low + RIM], pad, got[PIECE + low : PIECE + low + RIM], pad]
            box[c, FP:HP, HALF * half : HALF * half + HALF] = jnp.concatenate(rims, axis=0).astype(jnp.bfloat16)
        h_send[c] = dot(second_ref[...], box[c, 0:HP, :]).astype(jnp.bfloat16)
        on_sides((2, 3), lambda s: height_copy(s, c).start())

    def step_rows(c):
        on_sides((2, 3), lambda s: come(s, c))
        for s in (4, 5):
            for start, count, there in (TO_PREV, TO_NEXT)[s - 4]:
                at = there - (WN, WP)[s - 4] + 176 * (s - 4)
                w_send[c, at : at + count, :] = box[c, start : start + count, :]
        on_sides((4, 5), lambda s: width_copy(s, c).start())

    def step_attend(c):
        pl.when(c == 0)(lambda: arrive(load_attend))
        on_sides((4, 5), lambda s: come(s, c))
        edges = sum(jnp.where(present, 0, 1 << number) for number, _, _, present in sides)
        open_side = (side_ref[0:1, :] & edges) == 0
        queries, grads = load((q_ref, d_ref), 2, c)
        for g in range(GROUP):
            head = c * GROUP + g
            key_lanes = slice(g * HD, g * HD + HD)
            value_lanes = slice(HALF + g * HD, HALF + g * HD + HD)
            kind = (15 * ext[0, head] - 14) * (3 * ext[1, head] - 2) * ext[2, head]
            kinds = jnp.where(open_side, kind, 0)
            query, grad = queries[:, key_lanes], grads[:, key_lanes]
            key, value = box[c, :, key_lanes], box[c, :, value_lanes]
            scores = dot(query, key, ((1,), (1,)))
            scores = jnp.where((code_ref[...] & kinds) != 0, scores, -1e30)
            top = jnp.max(scores, axis=1, keepdims=True)
            raised = jnp.exp2((scores - top) * (SCALE * LOG2E))
            probs = raised * (1.0 / jnp.sum(raised, axis=1, keepdims=True))
            weights = probs.astype(jnp.bfloat16)
            attended = dot(weights, value).astype(jnp.bfloat16)
            rows_ref[4, :, key_lanes] = attended.astype(jnp.float32)
            delta = jnp.sum(grad.astype(jnp.float32) * attended.astype(jnp.float32), axis=1, keepdims=True)
            dprobs = dot(grad, value, ((1,), (1,)))
            dscores = (probs * (dprobs - delta) * SCALE).astype(jnp.bfloat16)
            rows_ref[5, :, key_lanes] = dot(dscores, key)
            key_part = dot(dscores, query, ((0,), (0,)))
            value_part = dot(weights, grad, ((0,), (0,)))
            for part, lanes in ((key_part, key_lanes), (value_part, value_lanes)):
                acc[c, :, lanes] = part[0:WP]
                w_back[c, :, lanes] = part[WP:PAD].astype(jnp.bfloat16)
        on_sides((4, 5), lambda s: back_copy(s, c).start())
        store((att_out, dq_out), 4, c)
        pl.when(c == CHUNKS - 1)(lambda: [leave(number, 0).start() for number in (0, 1)] and None)

    def step_back_columns(c):
        def take(s):
            come_back(s, c)
            for start, count, there in (TO_PREV, TO_NEXT)[s - 4]:
                low = there - (WN, WP)[s - 4] + 176 * (s - 4)
                acc[c, start : start + count, :] += w_got[c, low : low + count, :].astype(jnp.float32)

        on_sides((4, 5), take)
        h_back[c] = acc[c, HP:WP, :].astype(jnp.bfloat16)
        on_sides((2, 3), lambda s: back_copy(s, c).start())

    def step_back_rows(c):
        pl.when(c == 0)(lambda: arrive(load_back))
        on_sides((2, 3), lambda s: come_back(s, c))
        acc[c, 0:HP, :] += dot(second_t_ref[...], h_got[c])
        rims = [acc[c, low : low + RIM, HALF * half : HALF * half + HALF] for low in (FP, FN) for half in (0, 1)]
        f_back[c] = jnp.concatenate(rims, axis=0).astype(jnp.bfloat16)
        on_sides((0, 1), lambda s: frame_copies(1, s, c, lambda copy: copy.start()))

    def step_back_frames(c):
        on_sides((0, 1), lambda s: frames_come(1, s, c))
        got = f_got[c].astype(jnp.float32)
        halves = [jnp.concatenate([got[low : low + RIM], got[PIECE + low : PIECE + low + RIM]], axis=0) for low in (0, RIM)]
        terms = jnp.concatenate(halves, axis=1).astype(jnp.bfloat16)
        total = acc[c, 0:CELLS, :] + dot(frames_ref[...], terms)
        rows_ref[6] = total[:, 0:HALF]
        rows_ref[7] = total[:, HALF:LANES]
        store((dk_out, dv_out), 6, c)
        for number in (2, 3):
            leave(number, c).start()

    def tick(t, carry):
        for step, lag in zip(
            (
                step_first,
                functools.partial(step_forward, 0),
                step_frames,
                step_rows,
                step_attend,
                prepare,
                step_back_columns,
                step_back_rows,
                functools.partial(step_forward, 1),
                step_back_frames,
            ),
            LAG,
        ):
            c = t - lag
            pl.when((c >= max(0, -lag)) & (c < CHUNKS))(functools.partial(step, c))
        return carry

    arrive(load_first)
    prepare(0)
    pl.semaphore_wait(barrier, greeted)
    step_first(0)
    prepare(1)
    lax.fori_loop(0, CHUNKS + LAG[-1], tick, 0)
    for number in (0, 1):
        leave(number, 0).wait()

    def finish(c, carry):
        for number in (2, 3):
            leave(number, c).wait()
        on_sides(range(6), lambda s: all_sent(s, c))
        if shared:

            @pl.when((frame < low_mid) | (frame > high_mid))
            def _():
                for way in (0, 1):
                    forward(way, c, lambda copy: copy.wait_send())

        return carry

    lax.fori_loop(0, CHUNKS, finish, 0)


def hand_out(*refs):
    come, leave = [], []
    for i in range(4):
        for j in range(2):
            part = pl.ds(18 * j, 18)
            held = refs[8 + i].at[part]
            come.append(pltpu.make_async_copy(refs[i].at[part], held, refs[12].at[i, j]))
            leave.append(pltpu.make_async_copy(held, refs[4 + i].at[part], refs[13].at[i, j]))
    for copy in come:
        copy.start()
    for first, then in zip(come, leave):
        first.wait()
        then.start()
    for copy in leave:
        copy.wait()


def on_device(queries, keys, values, out_grad, extents):
    flat = [array.transpose(1, 2, 0, 3).reshape(36, 4, HEADS * HD) for array in (queries, keys, values, out_grad)]
    shape = jax.ShapeDtypeStruct((36, 4, HEADS * HD), jnp.bfloat16)
    vmem, place = pl.BlockSpec(memory_space=pltpu.VMEM), pl.BlockSpec(memory_space=pl.ANY)
    wide, narrow = LANES, HALF
    held = [(BOX, wide), (288, narrow), (288, narrow), (192, wide), (352, wide), (352, wide), (192, wide), (288, narrow)]
    held += [(352, wide), (192, wide), (288, narrow)]
    *tables_in, side = [jnp.asarray(table) for table in tables()]
    operands = [*flat, *tables_in]
    results = pl.pallas_call(
        kernel,
        out_shape=(shape,) * 4,
        in_specs=[pl.BlockSpec(memory_space=pltpu.SMEM), vmem] + [place] * 9,
        out_specs=(place,) * 4,
        scratch_shapes=[pltpu.VMEM(operand.shape, operand.dtype) for operand in operands]
        + [pltpu.VMEM(shape.shape, shape.dtype)] * 4
        + [pltpu.VMEM((CHUNKS, *dims), jnp.bfloat16) for dims in held]
        + [
            pltpu.VMEM((2, CHUNKS, RELAYED, HALF), jnp.bfloat16),
            pltpu.VMEM((CHUNKS, WP, LANES), jnp.float32),
            pltpu.VMEM((8, CELLS, HALF), jnp.float32),
            pltpu.SemaphoreType.DMA((20, CHUNKS)),
            pltpu.SemaphoreType.DMA((14, CHUNKS)),
            pltpu.SemaphoreType.DMA((9,)),
            pltpu.SemaphoreType.DMA((4, CHUNKS)),
        ],
        compiler_params=pltpu.CompilerParams(
            collective_id=0, has_side_effects=True, vmem_limit_bytes=60 * 1024 * 1024
        ),
        cost_estimate=pl.CostEstimate(flops=2_500_000_000, bytes_accessed=8_000_000, transcendentals=1_500_000),
    )(extents.T, side, *operands)
    results = pl.pallas_call(
        hand_out,
        out_shape=(shape,) * 4,
        in_specs=[place] * 4,
        out_specs=(place,) * 4,
        scratch_shapes=[pltpu.VMEM(shape.shape, shape.dtype)] * 4 + [pltpu.SemaphoreType.DMA((4, 2))] * 2,
        compiler_params=pltpu.CompilerParams(vmem_limit_bytes=60 * 1024 * 1024),
        cost_estimate=pl.CostEstimate(flops=0, bytes_accessed=3_600_000, transcendentals=0),
    )(*results)
    return tuple(result.reshape(6, 6, 4, HEADS * HD).transpose(2, 0, 1, 3) for result in results)


def solution(mesh):
    spec = P("frame", "height", "width", None)
    return jax.shard_map(
        on_device,
        mesh=mesh,
        in_specs=(spec, spec, spec, spec, P()),
        out_specs=(spec, spec, spec, spec),
        check_vma=False,
    )
```
